256 devices in a mesh: dom: 32 (over x, y, core), dest: 8 (over z).
Axes of the slice: x: 4, y: 4, z: 8, core: 2. Of those that a mesh axis runs over, the one named last changes fastest.
Arguments:
- cost: float32 [32768], P('dom'), may hold values from 0.2 to 1.5
- turn_weight: float32 [512, 64, 512], P('dom'), may hold values from 0.0005859375 to 0.01171875
- exit_value: float32 [384, 32768], P('dest', 'dom'), may hold values from 0.05 to 1
- demand: float32 [384, 32768], P('dest', 'dom'), may hold values from 0.02 to 1
- dest_weight: float32 [384], P('dest'), may hold values from 0.3 to 3
- slot_count: int32 [512], P('dom'), may hold values from 1 to 8
- col_ref: int32 [512, 8], P('dom'), may hold values from 0 to 79, as said below
- send_blocks: int32 [32, 32, 2], replicated, may hold values from 0 to 15
Outputs:
- flows: float32 [32768], P(('dom', 'dest'))
- cost_grad: float32 [32768], P(('dom', 'dest'))
The draws below stay inside these ranges and needn't reach their ends.
Inputs may be any that keep to these rules, and one draw needn't show every extreme that they name: `col_ref`: A value below 16 names a block of the row block's own partition; a value 16 + p * 2 + c names block send_blocks[p, o, c] of partition p, o being the row block's partition.
All inputs are finite; a program needn't handle non-finite values.
Results may differ from the reference program's by a relative error of at most 0.0001.
Values sent between devices are 32-bit elements; how exact they have to be, the bound alone decides.
A program may use at most 128 MiB of HBM per device.

```python
import math
import jax
import jax.numpy as jnp
from jax import lax

BLK = 64
SLOTS = 8
CAP = 2
NB_DEV = 16
DEST_DEV = 48
NBLK = 512
LINKS = 32768
DEST = 384
N_DOM = 32
N_DEST = 8


def draw_col_ref(key, part):
    kinds = jax.random.randint(jax.random.fold_in(key, 11), (NBLK, SLOTS), 0, 2)
    local_pick = jax.random.randint(jax.random.fold_in(key, 12), (NBLK, SLOTS), 0, NB_DEV)
    ghost_pick = jax.random.randint(jax.random.fold_in(key, 13), (NBLK, SLOTS), 0, N_DOM * CAP)
    refs = jnp.where(kinds == 0, local_pick, NB_DEV + ghost_pick)
    refs = refs.at[0, 0].set(NB_DEV + N_DOM * CAP - 1)
    refs = refs.at[0, 1].set(0)
    return refs.astype(jnp.int32)


def touch_ends(entries, stream_key, low, top_value):
    spot = [jax.random.randint(jax.random.fold_in(stream_key, axis), (), 0, length) for axis, length in enumerate(entries.shape)]
    longest = entries.shape.index(max(entries.shape))
    beside = spot[:longest] + [(spot[longest] + 1) % entries.shape[longest]] + spot[longest + 1:]
    return entries.at[tuple(spot)].set(low).at[tuple(beside)].set(top_value)


def steps_of(key, extent, shards, low, high):
    def one(axis_at, blocks):
        draws = jax.random.uniform(jax.random.fold_in(jax.random.fold_in(key, 6), axis_at), (blocks,), jnp.float32, low / len(shards), high / len(shards))
        return jnp.repeat(jnp.exp(draws), extent[axis_at] // blocks).reshape((-1,) + (1,) * (len(extent) - axis_at - 1))

    level = one(*shards[0])
    for cut in shards[1:]:
        level = level * one(*cut)
    return level


def setup_inputs(seed: int = 0) -> dict:
    key_of = jax.random.split(jax.random.key(seed), 9)
    cost = jnp.clip(0.2 + 1.3 * jax.random.uniform(key_of[0], (LINKS,), jnp.float32) ** steps_of(key_of[0], (LINKS,), ((0, 32),), -0.2, 0.2), 0.2, 1.5)
    turn_weight = jnp.clip(jnp.exp(math.log(0.01171875) - 2.9957322 * jax.random.uniform(key_of[1], (NBLK, BLK, SLOTS * BLK), jnp.float32) ** steps_of(key_of[1], (NBLK, BLK, SLOTS * BLK), ((0, 32),), -0.2, 0.2)), 0.0005859375, 0.01171875)
    exit_value = jnp.clip(jnp.exp(math.log(1.0) - 2.9957323 * jax.random.uniform(key_of[2], (DEST, LINKS), jnp.float32) ** steps_of(key_of[2], (DEST, LINKS), ((0, 8), (1, 32)), -0.2, 0.2)), 0.05, 1.0)
    demand = jnp.clip(jnp.exp(math.log(1.0) - 3.912023 * jax.random.uniform(key_of[3], (DEST, LINKS), jnp.float32) ** steps_of(key_of[3], (DEST, LINKS), ((0, 8), (1, 32)), -0.2, 0.2)), 0.02, 1.0)
    dest_weight = jnp.clip(jnp.exp(math.log(3.0) - 2.3025851 * jax.random.uniform(key_of[4], (DEST,), jnp.float32) ** steps_of(key_of[4], (DEST,), ((0, 8),), -0.2, 0.2)), 0.3, 3.0)
    slot_count = touch_ends(jax.random.randint(key_of[5], (NBLK,), 1, SLOTS + 1), jax.random.fold_in(key_of[5], 1), 1, SLOTS).astype(jnp.int32)
    col_ref = draw_col_ref(jax.random.fold_in(key_of[8], 71), 0)
    send_blocks = touch_ends(jax.random.randint(key_of[7], (N_DOM, N_DOM, CAP), 0, NB_DEV), jax.random.fold_in(key_of[7], 1), 0, NB_DEV - 1).astype(jnp.int32)
    return {"cost": cost, "turn_weight": turn_weight, "exit_value": exit_value, "demand": demand, "dest_weight": dest_weight, "slot_count": slot_count, "col_ref": col_ref, "send_blocks": send_blocks}


def global_columns(col_ref, send_blocks):
    owner = jnp.arange(NBLK, dtype=jnp.int32) // NB_DEV
    owner_grid = jnp.broadcast_to(owner[:, None], col_ref.shape)
    offset = jnp.maximum(col_ref - NB_DEV, 0)
    source = offset // CAP
    within = offset % CAP
    remote = source * NB_DEV + send_blocks[source, owner_grid, within]
    return jnp.where(col_ref < NB_DEV, owner_grid * NB_DEV + col_ref, remote).astype(jnp.int32)


def forward_product(field, turn_matrix, columns_global):
    rows = field.shape[0]
    picked = field.reshape(rows, NBLK, BLK)[:, columns_global, :]
    result = jnp.einsum("dnsj,nisj->dni", picked, turn_matrix, precision=lax.Precision.HIGHEST)
    return result.reshape(rows, LINKS)


def adjoint_product(field, turn_matrix, columns_global):
    rows = field.shape[0]
    terms = jnp.einsum("dni,nisj->dnsj", field.reshape(rows, NBLK, BLK), turn_matrix, precision=lax.Precision.HIGHEST)
    total = jnp.zeros((rows, NBLK, BLK), jnp.float32).at[:, columns_global, :].add(terms)
    return total.reshape(rows, LINKS)


def reference(cost, turn_weight, exit_value, demand, dest_weight, slot_count, col_ref, send_blocks):
    columns_global = global_columns(col_ref, send_blocks)
    live_slots = (jnp.arange(SLOTS, dtype=jnp.int32)[None, :] < slot_count[:, None]).astype(jnp.float32)
    turn_matrix = turn_weight.reshape(NBLK, BLK, SLOTS, BLK) * live_slots[:, None, :, None]
    link_scale = jnp.exp(-cost)

    def one_group(pieces):
        exit_part, demand_part, weight_part = pieces
        value = exit_part
        for sweep in range(2):
            value = forward_product(value * link_scale[None, :], turn_matrix, columns_global) + exit_part
        load = demand_part
        back = demand_part
        for sweep in range(2):
            ratio = load / value
            back = adjoint_product(ratio, turn_matrix, columns_global) * link_scale[None, :]
            load = value * back + demand_part
        return jnp.sum(load, axis=0), jnp.sum(weight_part[:, None] * value * back, axis=0)

    groups = (exit_value.reshape(N_DEST, DEST_DEV, LINKS), demand.reshape(N_DEST, DEST_DEV, LINKS), dest_weight.reshape(N_DEST, DEST_DEV))
    flow_parts, grad_parts = lax.map(one_group, groups)
    flows = jnp.sum(flow_parts, axis=0) / DEST
    cost_grad = -jnp.sum(grad_parts, axis=0) / DEST
    return flows, cost_grad
```

```python
import functools

import jax
import jax.numpy as jnp
from jax import lax
from jax.experimental import pallas as pl
from jax.experimental.pallas import tpu as pltpu
from jax.sharding import PartitionSpec as P

MESH = pl.DeviceIdType.MESH
BLK = 64
PAIR = 2 * BLK
SLOTS = 8
BLOCKS = 16
PARTS = 32
GROUPS = 8
DESTS = 48
CHUNKS = 2
ROWS = DESTS // CHUNKS
LIVE = BLOCKS * SLOTS
GHOSTS = 2 * PARTS
STAGES = 4


def hops(offset):
    dx, dy, dc = offset
    return min(dx, 4 - dx) + min(dy, 4 - dy) + 0.5 * dc


OFFSETS = sorted(
    ((dx, dy, dc) for dx in range(4) for dy in range(4) for dc in range(2) if dx or dy or dc),
    key=lambda o: -hops(o),
)
Z_OFFSETS = (4, 3, 5, 2, 6, 1, 7)


def split(v):
    high = v.astype(jnp.bfloat16)
    low = (v - high.astype(jnp.float32)).astype(jnp.bfloat16)
    return jnp.concatenate([high, low], axis=0)


def turn(v):
    return pltpu.roll(v, BLK, 1)


def kernel(
    cost_ref, exit_ref, demand_hbm, turn_hbm, weight_ref, count_ref, col_ref, outb_ref,
    flow_out, grad_out,
    turn_raw, demand_ref, matrix, table, exit_dup, weighted, value_dup, demand_dup, scale, dest_w,
    terms, scan, back_scan, local, returned, sort_v, sort_s,
    send, recv, z_part, z_recv,
    load_sem, send_sem, recv_sem, z_send_sem, z_recv_sem,
):
    me = lax.axis_index("dom")
    group = lax.axis_index("dest")
    x, y, c = me // 8, (me // 2) % 4, me % 2

    def partner(offset):
        dx, dy, dc = offset
        return (((x + dx) % 4) * 4 + (y + dy) % 4) * 2 + (c + dc) % 2

    barrier = pltpu.get_barrier_semaphore()
    for offset in OFFSETS:
        pl.semaphore_signal(barrier, inc=1, device_id=(partner(offset), group), device_id_type=MESH)
    for dz in Z_OFFSETS:
        pl.semaphore_signal(barrier, inc=1, device_id=(me, (group + dz) % GROUPS), device_id_type=MESH)

    turn_copy = pltpu.make_async_copy(turn_hbm, turn_raw, load_sem.at[0])
    turn_copy.start()
    demand_copy = pltpu.make_async_copy(demand_hbm, demand_ref, load_sem.at[1])
    demand_copy.start()

    lane = lax.broadcasted_iota(jnp.int32, (ROWS, PAIR), 1)
    low_half = lane < BLK
    half_of = lane // BLK
    low_half16 = lax.broadcasted_iota(jnp.int32, (2 * ROWS, PAIR), 1) < BLK

    def message(stage, chunk, make):
        for offset in OFFSETS:
            to = partner(offset)
            send[stage, chunk, to] = make(to)
            pltpu.make_async_remote_copy(
                src_ref=send.at[stage, chunk, to],
                dst_ref=recv.at[stage, chunk, me],
                send_sem=send_sem.at[stage, chunk],
                recv_sem=recv_sem.at[stage, chunk],
                device_id=(to, group),
                device_id_type=MESH,
            ).start()
        recv[stage, chunk, me] = make(me)

    def wait_received(stage, chunk):
        here = recv.at[stage, chunk, pl.ds(0, PARTS - 1)]
        pltpu.make_async_copy(here, here, recv_sem.at[stage, chunk]).wait()

    def forward_message(stage, chunk):
        def make(to):
            first, second = outb_ref[2 * to], outb_ref[2 * to + 1]
            return jnp.where(low_half, weighted[first], weighted[second])

        message(stage, chunk, make)

    def scale_row(n):
        return scale[n % 2, pl.ds(n // 2, 1), :]

    factor = jnp.exp(-cost_ref[...])
    turned = turn(factor)
    low8 = lax.broadcasted_iota(jnp.int32, (8, PAIR), 1) < BLK
    scale[0] = jnp.where(low8, factor, turned)
    scale[1] = jnp.where(low8, turned, factor)

    def rows_of(chunk):
        return pl.ds(pl.multiple_of(chunk * ROWS, 8), ROWS)

    def start_first(chunk):
        for m in range(BLOCKS // 2):
            pair = exit_ref[rows_of(chunk), m * PAIR : (m + 1) * PAIR]
            other = turn(pair)
            for h in range(2):
                dup = jnp.where(low_half, pair, other) if h == 0 else jnp.where(low_half, other, pair)
                exit_dup[chunk, 2 * m + h] = dup
                moved = dup * scale_row(2 * m + h)
                weighted[2 * m + h] = moved
                table[chunk, 2 * m + h] = split(moved)

    start_first(0)
    pl.semaphore_wait(barrier, len(OFFSETS) + len(Z_OFFSETS))
    forward_message(0, 0)

    @pl.loop(1, CHUNKS)
    def _(chunk):
        start_first(chunk)
        forward_message(0, chunk)

    turn_copy.wait()

    @pl.loop(0, BLOCKS)
    def _(n):
        column = lax.broadcasted_iota(jnp.int32, (BLK, SLOTS * BLK), 1)
        live = jnp.where(column < count_ref[n] * BLK, turn_raw[n], 0.0)
        matrix[n] = split(live)

    demand_copy.wait()

    @pl.loop(0, CHUNKS)
    def _(chunk):
        for m in range(BLOCKS // 2):
            pair = demand_ref[rows_of(chunk), m * PAIR : (m + 1) * PAIR]
            other = turn(pair)
            demand_dup[chunk, 2 * m] = jnp.where(low_half, pair, other)
            demand_dup[chunk, 2 * m + 1] = jnp.where(low_half, other, pair)

    @pl.loop(0, DESTS)
    def _(d):
        dest_w[pl.ds(d, 1), :] = jnp.full((1, PAIR), weight_ref[d], jnp.float32)

    square_lane = lax.broadcasted_iota(jnp.int32, (128, 128), 1)
    square_row = lax.broadcasted_iota(jnp.int32, (128, 128), 0)
    lane_row = lax.broadcasted_iota(jnp.int32, (1, 128), 1)

    def order(keys, total, at):
        def put(k, row):
            return jnp.where(lane_row == k, keys[k], row)

        row = lax.fori_loop(0, total, put, jnp.full((1, 128), 1000, jnp.int32))
        along = jnp.broadcast_to(row, (128, 128))
        down = along.T
        before = (along < down) | ((along == down) & (square_lane < square_row))
        rank = jnp.sum(jnp.where(before, 1, 0), axis=1, keepdims=True)
        hit = rank == square_lane
        entry = jnp.sum(jnp.where(hit, square_row, 0), axis=0, keepdims=True)
        key = jnp.sum(jnp.where(hit, down, 0), axis=0, keepdims=True)
        same = (key == pltpu.roll(key, 1, 1)) & (lane_row > 0)
        upto = jnp.sum(jnp.where(down <= square_lane, 1, 0), axis=0, keepdims=True)
        count = jnp.sum(jnp.where(down == square_lane, 1, 0), axis=0, keepdims=True)
        last = jnp.where(count > 0, upto - 1, total)
        sort_v[at : at + 1, :] = jnp.clip(entry, 0, total - 1)
        sort_v[at + 1 : at + 2, :] = jnp.where(same, 1, 0)
        sort_v[at + 2 : at + 3, :] = jnp.clip(last, 0, total)

    sort_v[...] = jnp.zeros_like(sort_v)
    order(col_ref, LIVE, 0)
    order(outb_ref, GHOSTS, 3)
    sort_copy = pltpu.make_async_copy(sort_v, sort_s, load_sem.at[2])
    sort_copy.start()
    sort_copy.wait()

    def run_sums(source, target, at, total):
        def step(k, running):
            entry = sort_s[at, k]
            found = jnp.where(half_of == entry % 2, source[entry // 2], 0.0)
            running = found + jnp.where(sort_s[at + 1, k] == 1, running, 0.0)
            target[k] = running
            return running

        lax.fori_loop(0, total, step, jnp.zeros((ROWS, PAIR), jnp.float32), unroll=8)

    scan[LIVE] = jnp.zeros((ROWS, PAIR), jnp.float32)
    back_scan[GHOSTS] = jnp.zeros((ROWS, PAIR), jnp.float32)

    def take_received(stage, chunk):
        @pl.loop(0, PARTS, unroll=4)
        def _(p):
            pair = recv[stage, chunk, p]
            other = turn(pair)
            table[chunk, BLOCKS + 2 * p] = split(jnp.where(low_half, pair, other))
            table[chunk, BLOCKS + 2 * p + 1] = split(jnp.where(low_half, other, pair))

    def product(chunk, n):
        picked = jnp.concatenate(
            [
                jnp.where(
                    low_half16,
                    table[chunk, col_ref[n * SLOTS + 2 * k]],
                    table[chunk, col_ref[n * SLOTS + 2 * k + 1]],
                )
                for k in range(SLOTS // 2)
            ],
            axis=1,
        )
        parts = lax.dot_general(
            picked, matrix[n], (((1,), (1,)), ((), ())), preferred_element_type=jnp.float32
        )
        both = parts[:ROWS] + parts[ROWS:]
        return both + turn(both)

    def adjoint_message(stage, chunk):
        run_sums(terms, scan, 0, LIVE)

        def make(to):
            first = scan[sort_s[2, BLOCKS + 2 * to]]
            second = scan[sort_s[2, BLOCKS + 2 * to + 1]]
            return jnp.where(low_half, first, second) + turn(jnp.where(low_half, second, first))

        message(stage, chunk, make)
        for b in range(BLOCKS):
            own = scan[sort_s[2, b]]
            local[chunk, b] = own + turn(own)

    def adjoint_product(n, ratio):
        parts = jnp.dot(split(ratio), matrix[n], preferred_element_type=jnp.float32)
        both = parts[:ROWS] + parts[ROWS:]
        for k in range(SLOTS // 2):
            terms[n * (SLOTS // 2) + k] = both[:, k * PAIR : (k + 1) * PAIR]

    @pl.loop(0, CHUNKS)
    def _(chunk):
        wait_received(0, chunk)
        take_received(0, chunk)
        for n in range(BLOCKS):
            value = product(chunk, n) + exit_dup[chunk, n]
            weighted[n] = value * scale_row(n)
        for n in range(BLOCKS):
            table[chunk, n] = split(weighted[n])
        forward_message(1, chunk)

    @pl.loop(0, CHUNKS)
    def _(chunk):
        wait_received(1, chunk)
        take_received(1, chunk)
        for n in range(BLOCKS):
            value = product(chunk, n) + exit_dup[chunk, n]
            value_dup[chunk, n] = value
            adjoint_product(n, demand_dup[chunk, n] / value)
        adjoint_message(2, chunk)

    def gather_back(stage, chunk):
        wait_received(stage, chunk)
        for p in range(PARTS):
            returned[p] = recv[stage, chunk, p]
        run_sums(returned, back_scan, 3, GHOSTS)

    def back_of(chunk, n):
        came = back_scan[sort_s[5, n]]
        return (local[chunk, n] + came + turn(came)) * scale_row(n)

    @pl.loop(0, CHUNKS)
    def _(chunk):
        gather_back(2, chunk)
        for n in range(BLOCKS):
            value = value_dup[chunk, n]
            load = value * back_of(chunk, n) + demand_dup[chunk, n]
            adjoint_product(n, load / value)
        adjoint_message(3, chunk)

    z_part[...] = jnp.zeros_like(z_part)
    low1 = lane_row < BLK

    @pl.loop(0, CHUNKS)
    def _(chunk):
        gather_back(3, chunk)
        weight = dest_w[rows_of(chunk), :]
        for g in range(GROUPS):
            flow, grad = [], []
            for h in range(2):
                n = 2 * g + h
                moved = value_dup[chunk, n] * back_of(chunk, n)
                flow.append(jnp.sum(moved + demand_dup[chunk, n], axis=0, keepdims=True))
                grad.append(jnp.sum(weight * moved, axis=0, keepdims=True))
            z_part[g, 0:1, :] += jnp.where(low1, flow[0], flow[1])
            z_part[g, 1:2, :] += jnp.where(low1, grad[0], grad[1])

    for dz in Z_OFFSETS:
        to = (group + dz) % GROUPS
        pltpu.make_async_remote_copy(
            src_ref=z_part.at[to],
            dst_ref=z_recv.at[group],
            send_sem=z_send_sem,
            recv_sem=z_recv_sem,
            device_id=(me, to),
            device_id_type=MESH,
        ).start()
    z_recv[group] = z_part[group]
    arrived = z_recv.at[pl.ds(0, GROUPS - 1)]
    pltpu.make_async_copy(arrived, arrived, z_recv_sem).wait()
    total = z_recv[0]
    for g in range(1, GROUPS):
        total = total + z_recv[g]
    total = total / (DESTS * GROUPS)
    flow_out[...] = total[0:1, :]
    grad_out[...] = -total[1:2, :]

    left = z_part.at[pl.ds(0, GROUPS - 1)]
    pltpu.make_async_copy(left, left, z_send_sem).wait()

    @pl.loop(0, STAGES)
    def _(stage):
        @pl.loop(0, CHUNKS)
        def _(chunk):
            gone = send.at[stage, chunk, pl.ds(0, PARTS - 1)]
            pltpu.make_async_copy(gone, gone, send_sem.at[stage, chunk]).wait()


def local_part(cost, turn_weight, exit_value, demand, dest_weight, slot_count, col_ref, send_blocks):
    me = lax.axis_index("dom")
    outbound = lax.dynamic_index_in_dim(send_blocks.reshape(PARTS, GHOSTS), me, 0, keepdims=False)
    vmem = pl.BlockSpec(memory_space=pltpu.VMEM)
    smem = pl.BlockSpec(memory_space=pltpu.SMEM)
    anywhere = pl.BlockSpec(memory_space=pl.ANY)
    f32, bf16 = jnp.float32, jnp.bfloat16
    flows, grad = pl.pallas_call(
        kernel,
        out_shape=(jax.ShapeDtypeStruct((1, PAIR), f32), jax.ShapeDtypeStruct((1, PAIR), f32)),
        in_specs=[vmem, vmem, anywhere, anywhere, smem, smem, smem, smem],
        out_specs=(vmem, vmem),
        scratch_shapes=[
            pltpu.VMEM((BLOCKS, BLK, SLOTS * BLK), f32),
            pltpu.VMEM((DESTS, BLOCKS * BLK), f32),
            pltpu.VMEM((BLOCKS, 2 * BLK, SLOTS * BLK), bf16),
            pltpu.VMEM((CHUNKS, BLOCKS + GHOSTS, 2 * ROWS, PAIR), bf16),
            pltpu.VMEM((CHUNKS, BLOCKS, ROWS, PAIR), f32),
            pltpu.VMEM((BLOCKS, ROWS, PAIR), f32),
            pltpu.VMEM((CHUNKS, BLOCKS, ROWS, PAIR), f32),
            pltpu.VMEM((CHUNKS, BLOCKS, ROWS, PAIR), f32),
            pltpu.VMEM((2, 8, PAIR), f32),
            pltpu.VMEM((DESTS, PAIR), f32),
            pltpu.VMEM((LIVE // 2, ROWS, PAIR), f32),
            pltpu.VMEM((LIVE + 1, ROWS, PAIR), f32),
            pltpu.VMEM((GHOSTS + 1, ROWS, PAIR), f32),
            pltpu.VMEM((CHUNKS, BLOCKS, ROWS, PAIR), f32),
            pltpu.VMEM((PARTS, ROWS, PAIR), f32),
            pltpu.VMEM((8, 128), jnp.int32),
            pltpu.SMEM((8, 128), jnp.int32),
            pltpu.VMEM((STAGES, CHUNKS, PARTS, ROWS, PAIR), f32),
            pltpu.VMEM((STAGES, CHUNKS, PARTS, ROWS, PAIR), f32),
            pltpu.VMEM((GROUPS, 8, PAIR), f32),
            pltpu.VMEM((GROUPS, 8, PAIR), f32),
            pltpu.SemaphoreType.DMA((3,)),
            pltpu.SemaphoreType.DMA((STAGES, CHUNKS)),
            pltpu.SemaphoreType.DMA((STAGES, CHUNKS)),
            pltpu.SemaphoreType.DMA,
            pltpu.SemaphoreType.DMA,
        ],
        compiler_params=pltpu.CompilerParams(
            collective_id=0, has_side_effects=True, vmem_limit_bytes=48 * 2**20
        ),
        name="route_choice",
    )(
        cost.reshape(8, PAIR), exit_value, demand, turn_weight, dest_weight, slot_count,
        col_ref.reshape(LIVE), outbound,
    )
    return flows.reshape(PAIR), grad.reshape(PAIR)


def solution(mesh):
    placed = (
        P("dom"),
        P("dom", None, None),
        P("dest", "dom"),
        P("dest", "dom"),
        P("dest"),
        P("dom"),
        P("dom", None),
        P(),
    )
    return jax.shard_map(
        local_part,
        mesh=mesh,
        in_specs=placed,
        out_specs=(P(("dom", "dest")), P(("dom", "dest"))),
        check_vma=False,
    )
```

```python
import functools

import jax
import jax.numpy as jnp
from jax import lax
from jax.experimental import pallas as pl
from jax.experimental.pallas import tpu as pltpu
from jax.sharding import PartitionSpec as P

MESH = pl.DeviceIdType.MESH
BLK = 64
PAIR = 2 * BLK
SLOTS = 8
BLOCKS = 16
PARTS = 32
GROUPS = 8
DESTS = 48
CHUNKS = 3
ROWS = DESTS // CHUNKS
LIVE = BLOCKS * SLOTS
GHOSTS = 2 * PARTS
STAGES = 4


def hops(offset):
    dx, dy, dc = offset
    return min(dx, 4 - dx) + min(dy, 4 - dy) + 0.5 * dc


OFFSETS = sorted(
    ((dx, dy, dc) for dx in range(4) for dy in range(4) for dc in range(2) if dx or dy or dc),
    key=lambda o: -hops(o),
)
Z_OFFSETS = (4, 3, 5, 2, 6, 1, 7)


def split(v):
    high = v.astype(jnp.bfloat16)
    low = (v - high.astype(jnp.float32)).astype(jnp.bfloat16)
    return jnp.concatenate([high, low], axis=0)


def turn(v):
    return pltpu.roll(v, BLK, 1)


def kernel(
    cost_hbm, exit_hbm, demand_hbm, turn_hbm, weight_hbm, count_hbm, col_hbm, send_blocks_hbm,
    flow_out, grad_out,
    turn_raw, exit_ref, demand_ref, cost_ref, weight_ref, count_ref, col_ref, outb_ref,
    matrix, across, table, picked, parts, ratios, exit_dup, weighted, value_dup, demand_dup, scale, dest_w,
    terms, scan, back_scan, keep, back_keep, local, returned, sort_v, sort_s,
    send, recv, z_part, z_recv,
    load_sem, send_sem, recv_sem, z_send_sem, z_recv_sem,
):
    me = lax.axis_index("dom")
    group = lax.axis_index("dest")
    x, y, c = me // 8, (me // 2) % 4, me % 2

    def partner(offset):
        dx, dy, dc = offset
        return (((x + dx) % 4) * 4 + (y + dy) % 4) * 2 + (c + dc) % 2

    loads = [
        pltpu.make_async_copy(source, target, load_sem.at[i])
        for i, (source, target) in enumerate(
            (
                (cost_hbm, cost_ref),
                (exit_hbm, exit_ref),
                (send_blocks_hbm.at[me], outb_ref),
                (turn_hbm, turn_raw),
                (demand_hbm, demand_ref),
                (col_hbm, col_ref),
                (count_hbm, count_ref),
                (weight_hbm, weight_ref),
            )
        )
    ]
    for load in loads:
        load.start()

    barrier = pltpu.get_barrier_semaphore()
    for offset in OFFSETS:
        pl.semaphore_signal(barrier, inc=1, device_id=(partner(offset), group), device_id_type=MESH)
    for dz in Z_OFFSETS:
        pl.semaphore_signal(barrier, inc=1, device_id=(me, (group + dz) % GROUPS), device_id_type=MESH)

    lane = lax.broadcasted_iota(jnp.int32, (ROWS, PAIR), 1)
    low_half = lane < BLK
    low_half16 = lax.broadcasted_iota(jnp.int32, (2 * ROWS, PAIR), 1) < BLK
    lane_row = lax.broadcasted_iota(jnp.int32, (1, PAIR), 1)
    low1 = lane_row < BLK

    def message(stage, chunk, make):
        for offset in OFFSETS:
            to = partner(offset)
            send[stage, chunk, to] = make(to)
            pltpu.make_async_remote_copy(
                src_ref=send.at[stage, chunk, to],
                dst_ref=recv.at[stage, chunk, me],
                send_sem=send_sem.at[stage, chunk],
                recv_sem=recv_sem.at[stage, chunk],
                device_id=(to, group),
                device_id_type=MESH,
            ).start()
        recv[stage, chunk, me] = make(me)

    def wait_received(stage, chunk):
        here = recv.at[stage, chunk, pl.ds(0, PARTS - 1)]
        pltpu.make_async_copy(here, here, recv_sem.at[stage, chunk]).wait()

    def forward_message(stage, chunk):
        def make(to):
            return jnp.where(low_half, weighted[outb_ref[0, to]], weighted[outb_ref[1, to]])

        message(stage, chunk, make)

    def scale_row(n):
        return scale[n : n + 1, :]

    def rows_of(chunk):
        return pl.ds(pl.multiple_of(chunk * ROWS, 8), ROWS)

    def start_first(chunk):
        for m in range(BLOCKS // 2):
            pair = exit_ref[rows_of(chunk), m * PAIR : (m + 1) * PAIR]
            other = turn(pair)
            for h in range(2):
                n = 2 * m + h
                dup = jnp.where(low_half, pair, other) if h == 0 else jnp.where(low_half, other, pair)
                exit_dup[chunk, n] = dup
                moved = dup * scale_row(n)
                weighted[n] = moved
                table[chunk, n] = split(moved)

    loads[0].wait()
    for m in range(BLOCKS // 2):
        factor = jnp.exp(-cost_ref[pl.ds(m * PAIR, PAIR)].reshape(1, PAIR))
        turned = turn(factor)
        scale[2 * m : 2 * m + 1, :] = jnp.where(low1, factor, turned)
        scale[2 * m + 1 : 2 * m + 2, :] = jnp.where(low1, turned, factor)
    loads[1].wait()
    loads[2].wait()
    start_first(0)
    pl.semaphore_wait(barrier, len(OFFSETS) + len(Z_OFFSETS))
    forward_message(0, 0)

    @pl.loop(1, CHUNKS)
    def _(chunk):
        start_first(chunk)
        forward_message(0, chunk)

    for load in loads[3:]:
        load.wait()

    square_lane = lax.broadcasted_iota(jnp.int32, (128, 128), 1)
    square_row = lax.broadcasted_iota(jnp.int32, (128, 128), 0)

    def order(keys, half, at, keep_ref):
        odd = lane_row >= half
        row = jnp.where(lane_row < 2 * half, keys + jnp.where(odd, 256, 0), 4096)
        along = jnp.broadcast_to(row, (128, 128))
        down = along.T
        before = (along < down) | ((along == down) & (square_lane < square_row))
        rank = jnp.sum(jnp.where(before, 1, 0), axis=1, keepdims=True)
        hit = rank == square_lane
        entry = jnp.sum(jnp.where(hit, square_row, 0), axis=0, keepdims=True)
        key = jnp.sum(jnp.where(hit, down, 0), axis=0, keepdims=True)
        same = (key == pltpu.roll(key, 1, 1)) & (lane_row > 0)
        kept = jnp.broadcast_to(jnp.where(same, 1.0, 0.0), (128, 128)).T
        keep_ref[...] = jnp.where(low1, kept[:half], kept[half : 2 * half])
        sort_v[at : at + 1, :] = jnp.clip(entry - jnp.where(odd, half, 0), 0, half - 1)
        for h in range(2):
            target = square_lane + 256 * h
            upto = jnp.sum(jnp.where(down <= target, 1, 0), axis=0, keepdims=True)
            count = jnp.sum(jnp.where(down == target, 1, 0), axis=0, keepdims=True)
            last = jnp.where(count > 0, upto - 1 - half * h, half)
            sort_v[at + 1 + h : at + 2 + h, :] = jnp.clip(last, 0, half)

    def col_key(n, row):
        for s in range(SLOTS):
            at = (s % 2) * (LIVE // 2) + n * (SLOTS // 2) + s // 2
            row = jnp.where(lane_row == at, col_ref[s, n], row)
        return row

    def out_key(q, row):
        for h in range(2):
            row = jnp.where(lane_row == h * PARTS + q, outb_ref[h, q], row)
        return row

    col_row = lax.fori_loop(0, BLOCKS, col_key, jnp.zeros((1, 128), jnp.int32))
    out_row = lax.fori_loop(0, PARTS, out_key, jnp.zeros((1, 128), jnp.int32))
    sort_v[...] = jnp.zeros_like(sort_v)
    order(col_row, LIVE // 2, 1, keep)
    order(out_row, PARTS, 4, back_keep)
    swapped = (col_row >= BLOCKS) & (lane_row >= LIVE // 2)
    sort_v[0:1, :] = jnp.where(swapped, col_row + 1 - 2 * (col_row % 2), col_row)
    sort_copy = pltpu.make_async_copy(sort_v, sort_s, load_sem.at[0])
    sort_copy.start()

    @pl.loop(0, BLOCKS)
    def _(n):
        column = lax.broadcasted_iota(jnp.int32, (BLK, SLOTS * BLK), 1)
        live = jnp.where(column < count_ref[n] * BLK, turn_raw[n], 0.0)
        both = split(live)
        matrix[n] = both
        across[n] = both.T

    @pl.loop(0, CHUNKS)
    def _(chunk):
        for m in range(BLOCKS // 2):
            pair = demand_ref[rows_of(chunk), m * PAIR : (m + 1) * PAIR]
            other = turn(pair)
            demand_dup[chunk, 2 * m] = jnp.where(low_half, pair, other)
            demand_dup[chunk, 2 * m + 1] = jnp.where(low_half, other, pair)

    @pl.loop(0, DESTS)
    def _(d):
        dest_w[pl.ds(d, 1), :] = jnp.full((1, PAIR), weight_ref[d], jnp.float32)

    sort_copy.wait()
    scan[LIVE // 2] = jnp.zeros((ROWS, PAIR), jnp.float32)
    back_scan[PARTS] = jnp.zeros((ROWS, PAIR), jnp.float32)
    z_part[...] = jnp.zeros_like(z_part)

    def run_sums(source, keep_ref, target, at, half):
        def step(k, running):
            even, odd = source[sort_s[at, k]], source[sort_s[at, half + k]]
            running = jnp.where(low_half, even, odd) + keep_ref[pl.ds(k, 1), :] * running
            target[k] = running
            return running

        lax.fori_loop(0, half, step, jnp.zeros((ROWS, PAIR), jnp.float32), unroll=16)

    def sums_at(source, at, first, second):
        return jnp.where(low_half, source[sort_s[at, first]], source[sort_s[at + 1, second]])

    def take_received(stage, chunk):
        @pl.loop(0, PARTS, unroll=8)
        def _(p):
            pair = recv[stage, chunk, p]
            table[chunk, BLOCKS + 2 * p] = split(pair)
            table[chunk, BLOCKS + 2 * p + 1] = split(turn(pair))

    def products(stage, chunk):
        wait_received(stage, chunk)
        take_received(stage, chunk)
        half = SLOTS // 2
        for n in range(BLOCKS):
            for k in range(half):
                even = table[chunk, sort_s[0, n * half + k]]
                odd = table[chunk, sort_s[0, LIVE // 2 + n * half + k]]
                picked[n, :, k * PAIR : (k + 1) * PAIR] = jnp.where(low_half16, even, odd)
        for n in range(BLOCKS):
            parts[n] = jnp.dot(picked[n], across[n], preferred_element_type=jnp.float32)

    def value_of(chunk, n):
        both = parts[n, :ROWS] + parts[n, ROWS:]
        return both + turn(both) + exit_dup[chunk, n]

    def adjoint_message(stage, chunk):
        half = SLOTS // 2
        for n in range(BLOCKS):
            out = jnp.dot(ratios[n], matrix[n], preferred_element_type=jnp.float32)
            both = out[:ROWS] + out[ROWS:]
            for k in range(half):
                terms[n * half + k] = both[:, k * PAIR : (k + 1) * PAIR]
        run_sums(terms, keep, scan, 1, LIVE // 2)

        def make(to):
            first = BLOCKS + 2 * to
            return sums_at(scan, 2, first, first + 1) + turn(sums_at(scan, 2, first + 1, first))

        message(stage, chunk, make)
        for b in range(BLOCKS):
            own = sums_at(scan, 2, b, b)
            local[chunk, b] = own + turn(own)

    @pl.loop(0, CHUNKS)
    def _(chunk):
        products(0, chunk)
        for n in range(BLOCKS):
            moved = value_of(chunk, n) * scale_row(n)
            weighted[n] = moved
            table[chunk, n] = split(moved)
        forward_message(1, chunk)

    @pl.loop(0, CHUNKS)
    def _(chunk):
        products(1, chunk)
        for n in range(BLOCKS):
            value = value_of(chunk, n)
            value_dup[chunk, n] = value
            ratios[n] = split(demand_dup[chunk, n] / value)
        adjoint_message(2, chunk)

    def gather_back(stage, chunk):
        wait_received(stage, chunk)
        for p in range(PARTS):
            returned[p] = recv[stage, chunk, p]
        run_sums(returned, back_keep, back_scan, 4, PARTS)

    def back_of(chunk, n):
        came = sums_at(back_scan, 5, n, n)
        return (local[chunk, n] + came + turn(came)) * scale_row(n)

    @pl.loop(0, CHUNKS)
    def _(chunk):
        gather_back(2, chunk)
        for n in range(BLOCKS):
            value = value_dup[chunk, n]
            load = value * back_of(chunk, n) + demand_dup[chunk, n]
            ratios[n] = split(load / value)
        adjoint_message(3, chunk)

    @pl.loop(0, CHUNKS)
    def _(chunk):
        gather_back(3, chunk)
        weight = dest_w[rows_of(chunk), :]
        for g in range(GROUPS):
            flow, grad = [], []
            for h in range(2):
                n = 2 * g + h
                moved = value_dup[chunk, n] * back_of(chunk, n)
                flow.append(jnp.sum(moved + demand_dup[chunk, n], axis=0, keepdims=True))
                grad.append(jnp.sum(weight * moved, axis=0, keepdims=True))
            z_part[g, 0:1, :] += jnp.where(low1, flow[0], flow[1])
            z_part[g, 1:2, :] += jnp.where(low1, grad[0], grad[1])

    for dz in Z_OFFSETS:
        to = (group + dz) % GROUPS
        pltpu.make_async_remote_copy(
            src_ref=z_part.at[to],
            dst_ref=z_recv.at[group],
            send_sem=z_send_sem,
            recv_sem=z_recv_sem,
            device_id=(me, to),
            device_id_type=MESH,
        ).start()
    z_recv[group] = z_part[group]
    arrived = z_recv.at[pl.ds(0, GROUPS - 1)]
    pltpu.make_async_copy(arrived, arrived, z_recv_sem).wait()
    total = z_recv[0]
    for g in range(1, GROUPS):
        total = total + z_recv[g]
    total = total / (DESTS * GROUPS)
    flow_out[...] = total[0:1, :]
    grad_out[...] = -total[1:2, :]

    left = z_part.at[pl.ds(0, GROUPS - 1)]
    pltpu.make_async_copy(left, left, z_send_sem).wait()

    @pl.loop(0, STAGES)
    def _(stage):
        @pl.loop(0, CHUNKS)
        def _(chunk):
            gone = send.at[stage, chunk, pl.ds(0, PARTS - 1)]
            pltpu.make_async_copy(gone, gone, send_sem.at[stage, chunk]).wait()


def local_part(cost, turn_weight, exit_value, demand, dest_weight, slot_count, col_ref, send_blocks):
    vmem = pl.BlockSpec(memory_space=pltpu.VMEM)
    anywhere = pl.BlockSpec(memory_space=pl.ANY)
    f32, bf16 = jnp.float32, jnp.bfloat16
    flows, grad = pl.pallas_call(
        kernel,
        out_shape=(jax.ShapeDtypeStruct((1, PAIR), f32), jax.ShapeDtypeStruct((1, PAIR), f32)),
        in_specs=[anywhere] * 8,
        out_specs=(vmem, vmem),
        scratch_shapes=[
            pltpu.VMEM((BLOCKS, BLK, SLOTS * BLK), f32),
            pltpu.VMEM((DESTS, BLOCKS * BLK), f32),
            pltpu.VMEM((DESTS, BLOCKS * BLK), f32),
            pltpu.VMEM((BLOCKS * BLK,), f32),
            pltpu.SMEM((DESTS,), f32),
            pltpu.SMEM((BLOCKS,), jnp.int32),
            pltpu.SMEM((SLOTS, BLOCKS), jnp.int32),
            pltpu.SMEM((2, PARTS), jnp.int32),
            pltpu.VMEM((BLOCKS, 2 * BLK, SLOTS * BLK), bf16),
            pltpu.VMEM((BLOCKS, SLOTS * BLK, 2 * BLK), bf16),
            pltpu.VMEM((CHUNKS, BLOCKS + GHOSTS, 2 * ROWS, PAIR), bf16),
            pltpu.VMEM((BLOCKS, 2 * ROWS, SLOTS * BLK), bf16),
            pltpu.VMEM((BLOCKS, 2 * ROWS, PAIR), f32),
            pltpu.VMEM((BLOCKS, 2 * ROWS, PAIR), bf16),
            pltpu.VMEM((CHUNKS, BLOCKS, ROWS, PAIR), f32),
            pltpu.VMEM((BLOCKS, ROWS, PAIR), f32),
            pltpu.VMEM((CHUNKS, BLOCKS, ROWS, PAIR), f32),
            pltpu.VMEM((CHUNKS, BLOCKS, ROWS, PAIR), f32),
            pltpu.VMEM((BLOCKS, PAIR), f32),
            pltpu.VMEM((DESTS, PAIR), f32),
            pltpu.VMEM((LIVE // 2, ROWS, PAIR), f32),
            pltpu.VMEM((LIVE // 2 + 1, ROWS, PAIR), f32),
            pltpu.VMEM((PARTS + 1, ROWS, PAIR), f32),
            pltpu.VMEM((LIVE // 2, PAIR), f32),
            pltpu.VMEM((PARTS, PAIR), f32),
            pltpu.VMEM((CHUNKS, BLOCKS, ROWS, PAIR), f32),
            pltpu.VMEM((PARTS, ROWS, PAIR), f32),
            pltpu.VMEM((8, 128), jnp.int32),
            pltpu.SMEM((8, 128), jnp.int32),
            pltpu.VMEM((STAGES, CHUNKS, PARTS, ROWS, PAIR), f32),
            pltpu.VMEM((STAGES, CHUNKS, PARTS, ROWS, PAIR), f32),
            pltpu.VMEM((GROUPS, 8, PAIR), f32),
            pltpu.VMEM((GROUPS, 8, PAIR), f32),
            pltpu.SemaphoreType.DMA((8,)),
            pltpu.SemaphoreType.DMA((STAGES, CHUNKS)),
            pltpu.SemaphoreType.DMA((STAGES, CHUNKS)),
            pltpu.SemaphoreType.DMA,
            pltpu.SemaphoreType.DMA,
        ],
        compiler_params=pltpu.CompilerParams(
            collective_id=0, has_side_effects=True, vmem_limit_bytes=60 * 2**20
        ),
        name="route_choice",
    )(
        cost, exit_value, demand, turn_weight, dest_weight, slot_count, col_ref.T,
        send_blocks.transpose(0, 2, 1),
    )
    return flows.reshape(PAIR), grad.reshape(PAIR)


def solution(mesh):
    placed = (
        P("dom"),
        P("dom", None, None),
        P("dest", "dom"),
        P("dest", "dom"),
        P("dest"),
        P("dom"),
        P("dom", None),
        P(),
    )
    return jax.shard_map(
        local_part,
        mesh=mesh,
        in_specs=placed,
        out_specs=(P(("dom", "dest")), P(("dom", "dest"))),
        check_vma=False,
    )
```

```python
import functools

import jax
import jax.numpy as jnp
from jax import lax
from jax.experimental import pallas as pl
from jax.experimental.pallas import tpu as pltpu
from jax.sharding import PartitionSpec as P

MESH = pl.DeviceIdType.MESH
BLK = 64
PAIR = 2 * BLK
SLOTS = 8
BLOCKS = 16
PARTS = 32
GROUPS = 8
DESTS = 48
CHUNKS = 3
ROWS = DESTS // CHUNKS
LIVE = BLOCKS * SLOTS
GHOSTS = 2 * PARTS
STAGES = 4


def hops(offset):
    dx, dy, dc = offset
    return min(dx, 4 - dx) + min(dy, 4 - dy) + 0.5 * dc


OFFSETS = sorted(
    ((dx, dy, dc) for dx in range(4) for dy in range(4) for dc in range(2) if dx or dy or dc),
    key=lambda o: -hops(o),
)
Z_OFFSETS = (4, 3, 5, 2, 6, 1, 7)


def split(v):
    high = v.astype(jnp.bfloat16)
    low = (v - high.astype(jnp.float32)).astype(jnp.bfloat16)
    return jnp.concatenate([high, low], axis=0)


def turn(v):
    return pltpu.roll(v, BLK, 1)


def kernel(
    cost_hbm, exit_hbm, demand_hbm, turn_hbm, weight_hbm, count_hbm, col_hbm, send_blocks_hbm,
    out_ref,
    turn_raw, exit_ref, demand_ref, cost_ref, weight_ref, count_ref, col_ref, outb_ref,
    matrix, across, table, picked, parts, ratios, exit_dup, weighted, value_dup, demand_dup, scale, dest_w,
    terms, scan, back_scan, keep, back_keep, local, returned, sort_v, sort_s, out_at, sum_at,
    send, recv, z_part, z_recv,
    load_sem, send_sem, recv_sem, z_send_sem, z_recv_sem,
):
    me = lax.axis_index("dom")
    group = lax.axis_index("dest")
    x, y, c = me // 8, (me // 2) % 4, me % 2

    along_x = [8 * ((x + d) % 4) for d in range(4)]
    along_y = [2 * ((y + d) % 4) for d in range(4)]
    core = (c, 1 - c)

    def partner(offset):
        dx, dy, dc = offset
        return along_x[dx] + along_y[dy] + core[dc]

    loads = [
        pltpu.make_async_copy(source, target, load_sem.at[i])
        for i, (source, target) in enumerate(
            (
                (cost_hbm, cost_ref),
                (exit_hbm, exit_ref),
                (send_blocks_hbm.at[me], outb_ref),
                (turn_hbm, turn_raw),
                (demand_hbm, demand_ref),
                (col_hbm, col_ref),
                (count_hbm, count_ref),
                (weight_hbm, weight_ref),
            )
        )
    ]
    for load in loads[:3]:
        load.start()

    barrier = pltpu.get_barrier_semaphore()
    for offset in OFFSETS:
        pl.semaphore_signal(barrier, inc=1, device_id=(partner(offset), group), device_id_type=MESH)
    for dz in Z_OFFSETS:
        pl.semaphore_signal(barrier, inc=1, device_id=(me, (group + dz) % GROUPS), device_id_type=MESH)

    for load in loads[3:]:
        load.start()

    lane = lax.broadcasted_iota(jnp.int32, (ROWS, PAIR), 1)
    low_half = lane < BLK
    low_half16 = lax.broadcasted_iota(jnp.int32, (2 * ROWS, PAIR), 1) < BLK
    lane_row = lax.broadcasted_iota(jnp.int32, (1, PAIR), 1)
    low1 = lane_row < BLK

    def message(stage, chunk, make):
        for i, offset in enumerate(OFFSETS):
            to = partner(offset)
            send[stage, chunk, i] = make(i)
            pltpu.make_async_remote_copy(
                src_ref=send.at[stage, chunk, i],
                dst_ref=recv.at[stage, chunk, me],
                send_sem=send_sem.at[stage, chunk],
                recv_sem=recv_sem.at[stage, chunk],
                device_id=(to, group),
                device_id_type=MESH,
            ).start()
        recv[stage, chunk, me] = make(PARTS - 1)

    def wait_received(stage, chunk):
        here = recv.at[stage, chunk, pl.ds(0, PARTS - 1)]
        pltpu.make_async_copy(here, here, recv_sem.at[stage, chunk]).wait()

    def forward_message(stage, chunk):
        def make(i):
            return jnp.where(low_half, weighted[out_at[2 * i]], weighted[out_at[2 * i + 1]])

        message(stage, chunk, make)

    def own_table(chunk):
        for n in range(BLOCKS):
            table[chunk, n] = split(weighted[n])

    def scale_row(n):
        return scale[n : n + 1, :]

    def rows_of(chunk):
        return pl.ds(pl.multiple_of(chunk * ROWS, 8), ROWS)

    def start_first(chunk):
        for m in range(BLOCKS // 2):
            pair = exit_ref[rows_of(chunk), m * PAIR : (m + 1) * PAIR]
            other = turn(pair)
            for h in range(2):
                n = 2 * m + h
                dup = jnp.where(low_half, pair, other) if h == 0 else jnp.where(low_half, other, pair)
                exit_dup[chunk, n] = dup
                weighted[n] = dup * scale_row(n)

    loads[0].wait()
    for m in range(BLOCKS // 2):
        factor = jnp.exp(-cost_ref[pl.ds(m * PAIR, PAIR)].reshape(1, PAIR))
        turned = turn(factor)
        scale[2 * m : 2 * m + 1, :] = jnp.where(low1, factor, turned)
        scale[2 * m + 1 : 2 * m + 2, :] = jnp.where(low1, turned, factor)
    loads[2].wait()
    for i, offset in enumerate((*OFFSETS, (0, 0, 0))):
        to = partner(offset)
        for h in range(2):
            out_at[2 * i + h] = outb_ref[h, to]
    loads[1].wait()
    start_first(0)
    pl.semaphore_wait(barrier, len(OFFSETS) + len(Z_OFFSETS))
    forward_message(0, 0)
    own_table(0)

    @pl.loop(1, CHUNKS)
    def _(chunk):
        start_first(chunk)
        forward_message(0, chunk)
        own_table(chunk)

    for load in loads[3:]:
        load.wait()

    square_lane = lax.broadcasted_iota(jnp.int32, (128, 128), 1)
    square_row = lax.broadcasted_iota(jnp.int32, (128, 128), 0)

    def order(keys, half, at, keep_ref):
        odd = lane_row >= half
        row = jnp.where(lane_row < 2 * half, keys + jnp.where(odd, 256, 0), 4096)
        along = jnp.broadcast_to(row, (128, 128))
        down = along.T
        before = (along < down) | ((along == down) & (square_lane < square_row))
        rank = jnp.sum(jnp.where(before, 1, 0), axis=1, keepdims=True)
        hit = rank == square_lane
        entry = jnp.sum(jnp.where(hit, square_row, 0), axis=0, keepdims=True)
        key = jnp.sum(jnp.where(hit, down, 0), axis=0, keepdims=True)
        same = (key == pltpu.roll(key, 1, 1)) & (lane_row > 0)
        kept = jnp.broadcast_to(jnp.where(same, 1.0, 0.0), (128, 128)).T
        keep_ref[...] = jnp.where(low1, kept[:half], kept[half : 2 * half])
        sort_v[at : at + 1, :] = jnp.clip(entry - jnp.where(odd, half, 0), 0, half - 1)
        for h in range(2):
            target = square_lane + 256 * h
            upto = jnp.sum(jnp.where(down <= target, 1, 0), axis=0, keepdims=True)
            count = jnp.sum(jnp.where(down == target, 1, 0), axis=0, keepdims=True)
            last = jnp.where(count > 0, upto - 1 - half * h, half)
            sort_v[at + 1 + h : at + 2 + h, :] = jnp.clip(last, 0, half)

    def col_key(n, row):
        for s in range(SLOTS):
            at = (s % 2) * (LIVE // 2) + n * (SLOTS // 2) + s // 2
            row = jnp.where(lane_row == at, col_ref[s, n], row)
        return row

    def out_key(q, row):
        for h in range(2):
            row = jnp.where(lane_row == h * PARTS + q, outb_ref[h, q], row)
        return row

    col_row = lax.fori_loop(0, BLOCKS, col_key, jnp.zeros((1, 128), jnp.int32))
    out_row = lax.fori_loop(0, PARTS, out_key, jnp.zeros((1, 128), jnp.int32))
    sort_v[...] = jnp.zeros_like(sort_v)
    order(col_row, LIVE // 2, 1, keep)
    order(out_row, PARTS, 4, back_keep)
    swapped = (col_row >= BLOCKS) & (lane_row >= LIVE // 2)
    sort_v[0:1, :] = jnp.where(swapped, col_row + 1 - 2 * (col_row % 2), col_row)
    sort_copy = pltpu.make_async_copy(sort_v, sort_s, load_sem.at[0])
    sort_copy.start()

    @pl.loop(0, BLOCKS)
    def _(n):
        column = lax.broadcasted_iota(jnp.int32, (BLK, SLOTS * BLK), 1)
        live = jnp.where(column < count_ref[n] * BLK, turn_raw[n], 0.0)
        both = split(live)
        matrix[n] = both
        across[n] = both.T

    @pl.loop(0, CHUNKS)
    def _(chunk):
        for m in range(BLOCKS // 2):
            pair = demand_ref[rows_of(chunk), m * PAIR : (m + 1) * PAIR]
            other = turn(pair)
            demand_dup[chunk, 2 * m] = jnp.where(low_half, pair, other)
            demand_dup[chunk, 2 * m + 1] = jnp.where(low_half, other, pair)

    @pl.loop(0, DESTS)
    def _(d):
        dest_w[pl.ds(d, 1), :] = jnp.full((1, PAIR), weight_ref[d], jnp.float32)

    sort_copy.wait()
    for i, offset in enumerate((*OFFSETS, (0, 0, 0))):
        first = BLOCKS + 2 * partner(offset)
        sum_at[4 * i] = sort_s[2, first]
        sum_at[4 * i + 1] = sort_s[3, first + 1]
        sum_at[4 * i + 2] = sort_s[2, first + 1]
        sum_at[4 * i + 3] = sort_s[3, first]
    scan[LIVE // 2] = jnp.zeros((ROWS, PAIR), jnp.float32)
    back_scan[PARTS] = jnp.zeros((ROWS, PAIR), jnp.float32)
    z_part[...] = jnp.zeros_like(z_part)

    def run_sums(source, keep_ref, target, at, half):
        for k in range(half):
            found = jnp.where(low_half, source[sort_s[at, k]], source[sort_s[at, half + k]])
            running = found if k == 0 else found + keep_ref[k : k + 1, :] * running
            target[k] = running

    def sums_at(source, at, first, second):
        return jnp.where(low_half, source[sort_s[at, first]], source[sort_s[at + 1, second]])

    def take_received(stage, chunk):
        @pl.loop(0, PARTS, unroll=8)
        def _(p):
            pair = recv[stage, chunk, p]
            table[chunk, BLOCKS + 2 * p] = split(pair)
            table[chunk, BLOCKS + 2 * p + 1] = split(turn(pair))

    def products(stage, chunk):
        wait_received(stage, chunk)
        take_received(stage, chunk)
        half = SLOTS // 2
        for n in range(BLOCKS):
            for k in range(half):
                even = table[chunk, sort_s[0, n * half + k]]
                odd = table[chunk, sort_s[0, LIVE // 2 + n * half + k]]
                picked[n, :, k * PAIR : (k + 1) * PAIR] = jnp.where(low_half16, even, odd)
        for n in range(BLOCKS):
            parts[n] = jnp.dot(picked[n], across[n], preferred_element_type=jnp.float32)

    def value_of(chunk, n):
        both = parts[n, :ROWS] + parts[n, ROWS:]
        return both + turn(both) + exit_dup[chunk, n]

    def adjoint_message(stage, chunk):
        half = SLOTS // 2
        for n in range(BLOCKS):
            out = jnp.dot(ratios[n], matrix[n], preferred_element_type=jnp.float32)
            both = out[:ROWS] + out[ROWS:]
            for k in range(half):
                terms[n * half + k] = both[:, k * PAIR : (k + 1) * PAIR]
        run_sums(terms, keep, scan, 1, LIVE // 2)

        def make(i):
            one, two, three, four = (scan[sum_at[4 * i + j]] for j in range(4))
            return jnp.where(low_half, one, two) + turn(jnp.where(low_half, three, four))

        message(stage, chunk, make)
        for b in range(BLOCKS):
            own = sums_at(scan, 2, b, b)
            local[chunk, b] = own + turn(own)

    @pl.loop(0, CHUNKS)
    def _(chunk):
        products(0, chunk)
        for n in range(BLOCKS):
            weighted[n] = value_of(chunk, n) * scale_row(n)
        forward_message(1, chunk)
        own_table(chunk)

    @pl.loop(0, CHUNKS)
    def _(chunk):
        products(1, chunk)
        for n in range(BLOCKS):
            value = value_of(chunk, n)
            value_dup[chunk, n] = value
            ratios[n] = split(demand_dup[chunk, n] / value)
        adjoint_message(2, chunk)

    def gather_back(stage, chunk):
        wait_received(stage, chunk)
        for p in range(PARTS):
            returned[p] = recv[stage, chunk, p]
        run_sums(returned, back_keep, back_scan, 4, PARTS)

    def back_of(chunk, n):
        came = sums_at(back_scan, 5, n, n)
        return (local[chunk, n] + came + turn(came)) * scale_row(n)

    @pl.loop(0, CHUNKS)
    def _(chunk):
        gather_back(2, chunk)
        for n in range(BLOCKS):
            value = value_dup[chunk, n]
            load = value * back_of(chunk, n) + demand_dup[chunk, n]
            ratios[n] = split(load / value)
        adjoint_message(3, chunk)

    @pl.loop(0, CHUNKS)
    def _(chunk):
        gather_back(3, chunk)
        weight = dest_w[rows_of(chunk), :]
        for g in range(GROUPS):
            flow, grad = [], []
            for h in range(2):
                n = 2 * g + h
                moved = value_dup[chunk, n] * back_of(chunk, n)
                flow.append(jnp.sum(moved + demand_dup[chunk, n], axis=0, keepdims=True))
                grad.append(jnp.sum(weight * moved, axis=0, keepdims=True))
            z_part[g, 0:1, :] += jnp.where(low1, flow[0], flow[1])
            z_part[g, 1:2, :] += jnp.where(low1, grad[0], grad[1])

    for dz in Z_OFFSETS:
        to = (group + dz) % GROUPS
        pltpu.make_async_remote_copy(
            src_ref=z_part.at[to],
            dst_ref=z_recv.at[group],
            send_sem=z_send_sem,
            recv_sem=z_recv_sem,
            device_id=(me, to),
            device_id_type=MESH,
        ).start()
    z_recv[group] = z_part[group]
    arrived = z_recv.at[pl.ds(0, GROUPS - 1)]
    pltpu.make_async_copy(arrived, arrived, z_recv_sem).wait()
    total = z_recv[0]
    for g in range(1, GROUPS):
        total = total + z_recv[g]
    out_ref[...] = total / (DESTS * GROUPS)

    left = z_part.at[pl.ds(0, GROUPS - 1)]
    pltpu.make_async_copy(left, left, z_send_sem).wait()

    @pl.loop(0, STAGES)
    def _(stage):
        @pl.loop(0, CHUNKS)
        def _(chunk):
            gone = send.at[stage, chunk, pl.ds(0, PARTS - 1)]
            pltpu.make_async_copy(gone, gone, send_sem.at[stage, chunk]).wait()


def local_part(cost, turn_weight, exit_value, demand, dest_weight, slot_count, col_ref, send_blocks):
    vmem = pl.BlockSpec(memory_space=pltpu.VMEM)
    anywhere = pl.BlockSpec(memory_space=pl.ANY)
    f32, bf16 = jnp.float32, jnp.bfloat16
    both = pl.pallas_call(
        kernel,
        out_shape=jax.ShapeDtypeStruct((8, PAIR), f32),
        in_specs=[anywhere] * 8,
        out_specs=vmem,
        scratch_shapes=[
            pltpu.VMEM((BLOCKS, BLK, SLOTS * BLK), f32),
            pltpu.VMEM((DESTS, BLOCKS * BLK), f32),
            pltpu.VMEM((DESTS, BLOCKS * BLK), f32),
            pltpu.VMEM((BLOCKS * BLK,), f32),
            pltpu.SMEM((DESTS,), f32),
            pltpu.SMEM((BLOCKS,), jnp.int32),
            pltpu.SMEM((SLOTS, BLOCKS), jnp.int32),
            pltpu.SMEM((2, PARTS), jnp.int32),
            pltpu.VMEM((BLOCKS, 2 * BLK, SLOTS * BLK), bf16),
            pltpu.VMEM((BLOCKS, SLOTS * BLK, 2 * BLK), bf16),
            pltpu.VMEM((CHUNKS, BLOCKS + GHOSTS, 2 * ROWS, PAIR), bf16),
            pltpu.VMEM((BLOCKS, 2 * ROWS, SLOTS * BLK), bf16),
            pltpu.VMEM((BLOCKS, 2 * ROWS, PAIR), f32),
            pltpu.VMEM((BLOCKS, 2 * ROWS, PAIR), bf16),
            pltpu.VMEM((CHUNKS, BLOCKS, ROWS, PAIR), f32),
            pltpu.VMEM((BLOCKS, ROWS, PAIR), f32),
            pltpu.VMEM((CHUNKS, BLOCKS, ROWS, PAIR), f32),
            pltpu.VMEM((CHUNKS, BLOCKS, ROWS, PAIR), f32),
            pltpu.VMEM((BLOCKS, PAIR), f32),
            pltpu.VMEM((DESTS, PAIR), f32),
            pltpu.VMEM((LIVE // 2, ROWS, PAIR), f32),
            pltpu.VMEM((LIVE // 2 + 1, ROWS, PAIR), f32),
            pltpu.VMEM((PARTS + 1, ROWS, PAIR), f32),
            pltpu.VMEM((LIVE // 2, PAIR), f32),
            pltpu.VMEM((PARTS, PAIR), f32),
            pltpu.VMEM((CHUNKS, BLOCKS, ROWS, PAIR), f32),
            pltpu.VMEM((PARTS, ROWS, PAIR), f32),
            pltpu.VMEM((8, 128), jnp.int32),
            pltpu.SMEM((8, 128), jnp.int32),
            pltpu.SMEM((2 * PARTS,), jnp.int32),
            pltpu.SMEM((4 * PARTS,), jnp.int32),
            pltpu.VMEM((STAGES, CHUNKS, PARTS, ROWS, PAIR), f32),
            pltpu.VMEM((STAGES, CHUNKS, PARTS, ROWS, PAIR), f32),
            pltpu.VMEM((GROUPS, 8, PAIR), f32),
            pltpu.VMEM((GROUPS, 8, PAIR), f32),
            pltpu.SemaphoreType.DMA((8,)),
            pltpu.SemaphoreType.DMA((STAGES, CHUNKS)),
            pltpu.SemaphoreType.DMA((STAGES, CHUNKS)),
            pltpu.SemaphoreType.DMA,
            pltpu.SemaphoreType.DMA,
        ],
        compiler_params=pltpu.CompilerParams(
            collective_id=0, has_side_effects=True, vmem_limit_bytes=60 * 2**20
        ),
        name="route_choice",
    )(
        cost, exit_value, demand, turn_weight, dest_weight, slot_count, col_ref.T,
        send_blocks.transpose(0, 2, 1),
    )
    return both[0], -both[1]


def solution(mesh):
    placed = (
        P("dom"),
        P("dom", None, None),
        P("dest", "dom"),
        P("dest", "dom"),
        P("dest"),
        P("dom"),
        P("dom", None),
        P(),
    )
    return jax.shard_map(
        local_part,
        mesh=mesh,
        in_specs=placed,
        out_specs=(P(("dom", "dest")), P(("dom", "dest"))),
        check_vma=False,
    )
```

```python
import functools

import jax
import jax.numpy as jnp
from jax import lax
from jax.experimental import pallas as pl
from jax.experimental.pallas import tpu as pltpu
from jax.sharding import PartitionSpec as P

MESH = pl.DeviceIdType.MESH
BLK = 64
PAIR = 2 * BLK
SLOTS = 8
BLOCKS = 16
PARTS = 32
GROUPS = 8
DESTS = 48
CHUNKS = 3
ROWS = DESTS // CHUNKS
LIVE = BLOCKS * SLOTS
GHOSTS = 2 * PARTS
STAGES = 4


def hops(offset):
    dx, dy, dc = offset
    return min(dx, 4 - dx) + min(dy, 4 - dy) + 0.5 * dc


OFFSETS = sorted(
    ((dx, dy, dc) for dx in range(4) for dy in range(4) for dc in range(2) if dx or dy or dc),
    key=lambda o: -hops(o),
)
Z_OFFSETS = (4, 3, 5, 2, 6, 1, 7)


def split(v):
    high = v.astype(jnp.bfloat16)
    low = (v - high.astype(jnp.float32)).astype(jnp.bfloat16)
    return jnp.concatenate([high, low], axis=0)


def turn(v):
    return pltpu.roll(v, BLK, 1)


def kernel(
    cost_hbm, exit_hbm, demand_hbm, turn_hbm, weight_hbm, count_hbm, col_hbm, send_blocks_hbm,
    z_out,
    turn_raw, exit_ref, demand_ref, cost_ref, weight_ref, count_ref, col_ref, outb_ref,
    matrix, across, table, picked, parts, ratios, exit_dup, weighted, value_dup, ratio_dup, demand_dup, scale, dest_w,
    terms, scan, back_scan, keep, back_keep, local, returned, sort_v, sort_s, out_at, sum_at,
    send, recv, z_part,
    load_sem, send_sem, recv_sem, z_send_sem, z_recv_sem, z_own_sem,
):
    me = lax.axis_index("dom")
    group = lax.axis_index("dest")
    x, y, c = me // 8, (me // 2) % 4, me % 2

    along_x = [8 * ((x + d) % 4) for d in range(4)]
    along_y = [2 * ((y + d) % 4) for d in range(4)]
    core = (c, 1 - c)

    def partner(offset):
        dx, dy, dc = offset
        return along_x[dx] + along_y[dy] + core[dc]

    loads = [
        pltpu.make_async_copy(source, target, load_sem.at[i])
        for i, (source, target) in enumerate(
            (
                (cost_hbm, cost_ref),
                (exit_hbm, exit_ref),
                (send_blocks_hbm.at[me], outb_ref),
                (turn_hbm, turn_raw),
                (demand_hbm, demand_ref),
                (col_hbm, col_ref),
                (count_hbm, count_ref),
                (weight_hbm, weight_ref),
            )
        )
    ]
    for load in loads[:3]:
        load.start()

    barrier = pltpu.get_barrier_semaphore()
    for offset in OFFSETS:
        pl.semaphore_signal(barrier, inc=1, device_id=(partner(offset), group), device_id_type=MESH)
    for dz in Z_OFFSETS:
        pl.semaphore_signal(barrier, inc=1, device_id=(me, (group + dz) % GROUPS), device_id_type=MESH)

    for load in loads[3:]:
        load.start()

    lane = lax.broadcasted_iota(jnp.int32, (ROWS, PAIR), 1)
    low_half = lane < BLK
    low_half16 = lax.broadcasted_iota(jnp.int32, (2 * ROWS, PAIR), 1) < BLK
    lane_row = lax.broadcasted_iota(jnp.int32, (1, PAIR), 1)
    low1 = lane_row < BLK

    def message(stage, chunk, make):
        for i, offset in enumerate(OFFSETS):
            to = partner(offset)
            send[stage, chunk, i] = make(i)
            pltpu.make_async_remote_copy(
                src_ref=send.at[stage, chunk, i],
                dst_ref=recv.at[stage, chunk, me],
                send_sem=send_sem.at[stage, chunk],
                recv_sem=recv_sem.at[stage, chunk],
                device_id=(to, group),
                device_id_type=MESH,
            ).start()
        recv[stage, chunk, me] = make(PARTS - 1)

    def wait_received(stage, chunk):
        here = recv.at[stage, chunk, pl.ds(0, PARTS - 1)]
        pltpu.make_async_copy(here, here, recv_sem.at[stage, chunk]).wait()

    def forward_message(stage, chunk):
        def make(i):
            return jnp.where(low_half, weighted[out_at[2 * i]], weighted[out_at[2 * i + 1]])

        message(stage, chunk, make)

    def own_table(chunk):
        for n in range(BLOCKS):
            table[chunk, n] = split(weighted[n])

    def scale_row(n):
        return scale[n : n + 1, :]

    def rows_of(chunk):
        return pl.ds(pl.multiple_of(chunk * ROWS, 8), ROWS)

    def start_first(chunk):
        for m in range(BLOCKS // 2):
            pair = exit_ref[rows_of(chunk), m * PAIR : (m + 1) * PAIR]
            other = turn(pair)
            for h in range(2):
                n = 2 * m + h
                dup = jnp.where(low_half, pair, other) if h == 0 else jnp.where(low_half, other, pair)
                exit_dup[chunk, n] = dup
                weighted[n] = dup * scale_row(n)

    loads[0].wait()
    for m in range(BLOCKS // 2):
        factor = jnp.exp(-cost_ref[pl.ds(m * PAIR, PAIR)].reshape(1, PAIR))
        turned = turn(factor)
        scale[2 * m : 2 * m + 1, :] = jnp.where(low1, factor, turned)
        scale[2 * m + 1 : 2 * m + 2, :] = jnp.where(low1, turned, factor)
    loads[2].wait()
    for i, offset in enumerate((*OFFSETS, (0, 0, 0))):
        to = partner(offset)
        for h in range(2):
            out_at[2 * i + h] = outb_ref[h, to]
    loads[1].wait()
    start_first(0)
    pl.semaphore_wait(barrier, len(OFFSETS) + len(Z_OFFSETS))
    forward_message(0, 0)
    own_table(0)

    @pl.loop(1, CHUNKS)
    def _(chunk):
        start_first(chunk)
        forward_message(0, chunk)
        own_table(chunk)

    for load in loads[3:]:
        load.wait()

    square_lane = lax.broadcasted_iota(jnp.int32, (128, 128), 1)
    square_row = lax.broadcasted_iota(jnp.int32, (128, 128), 0)

    def order(keys, half, at, keep_ref):
        odd = lane_row >= half
        row = jnp.where(lane_row < 2 * half, keys + jnp.where(odd, 256, 0), 4096)
        along = jnp.broadcast_to(row, (128, 128))
        down = along.T
        before = (along < down) | ((along == down) & (square_lane < square_row))
        rank = jnp.sum(jnp.where(before, 1, 0), axis=1, keepdims=True)
        hit = rank == square_lane
        entry = jnp.sum(jnp.where(hit, square_row, 0), axis=0, keepdims=True)
        key = jnp.sum(jnp.where(hit, down, 0), axis=0, keepdims=True)
        same = (key == pltpu.roll(key, 1, 1)) & (lane_row > 0)
        kept = jnp.broadcast_to(jnp.where(same, 1.0, 0.0), (128, 128)).T
        keep_ref[...] = jnp.where(low1, kept[:half], kept[half : 2 * half])
        sort_v[at : at + 1, :] = jnp.clip(entry - jnp.where(odd, half, 0), 0, half - 1)
        for h in range(2):
            target = square_lane + 256 * h
            upto = jnp.sum(jnp.where(down <= target, 1, 0), axis=0, keepdims=True)
            count = jnp.sum(jnp.where(down == target, 1, 0), axis=0, keepdims=True)
            last = jnp.where(count > 0, upto - 1 - half * h, half)
            sort_v[at + 1 + h : at + 2 + h, :] = jnp.clip(last, 0, half)

    def col_key(n, row):
        for s in range(SLOTS):
            at = (s % 2) * (LIVE // 2) + n * (SLOTS // 2) + s // 2
            row = jnp.where(lane_row == at, col_ref[s, n], row)
        return row

    def out_key(q, row):
        for h in range(2):
            row = jnp.where(lane_row == h * PARTS + q, outb_ref[h, q], row)
        return row

    col_row = lax.fori_loop(0, BLOCKS, col_key, jnp.zeros((1, 128), jnp.int32))
    out_row = lax.fori_loop(0, PARTS, out_key, jnp.zeros((1, 128), jnp.int32))
    sort_v[...] = jnp.zeros_like(sort_v)
    order(col_row, LIVE // 2, 1, keep)
    order(out_row, PARTS, 4, back_keep)
    swapped = (col_row >= BLOCKS) & (lane_row >= LIVE // 2)
    sort_v[0:1, :] = jnp.where(swapped, col_row + 1 - 2 * (col_row % 2), col_row)
    sort_copy = pltpu.make_async_copy(sort_v, sort_s, load_sem.at[0])
    sort_copy.start()

    @pl.loop(0, BLOCKS)
    def _(n):
        column = lax.broadcasted_iota(jnp.int32, (BLK, SLOTS * BLK), 1)
        live = jnp.where(column < count_ref[n] * BLK, turn_raw[n], 0.0)
        both = split(live)
        matrix[n] = both
        across[n] = both.T

    @pl.loop(0, CHUNKS)
    def _(chunk):
        for m in range(BLOCKS // 2):
            pair = demand_ref[rows_of(chunk), m * PAIR : (m + 1) * PAIR]
            other = turn(pair)
            demand_dup[chunk, 2 * m] = jnp.where(low_half, pair, other)
            demand_dup[chunk, 2 * m + 1] = jnp.where(low_half, other, pair)

    @pl.loop(0, DESTS)
    def _(d):
        dest_w[pl.ds(d, 1), :] = jnp.full((1, PAIR), weight_ref[d], jnp.float32)

    sort_copy.wait()
    for i, offset in enumerate((*OFFSETS, (0, 0, 0))):
        first = BLOCKS + 2 * partner(offset)
        sum_at[4 * i] = sort_s[2, first]
        sum_at[4 * i + 1] = sort_s[3, first + 1]
        sum_at[4 * i + 2] = sort_s[2, first + 1]
        sum_at[4 * i + 3] = sort_s[3, first]
    scan[LIVE // 2] = jnp.zeros((ROWS, PAIR), jnp.float32)
    back_scan[PARTS] = jnp.zeros((ROWS, PAIR), jnp.float32)
    z_part[...] = jnp.zeros_like(z_part)

    def run_sums(source, keep_ref, target, at, half):
        for k in range(half):
            found = jnp.where(low_half, source[sort_s[at, k]], source[sort_s[at, half + k]])
            running = found if k == 0 else found + keep_ref[k : k + 1, :] * running
            target[k] = running

    def sums_at(source, at, first, second):
        return jnp.where(low_half, source[sort_s[at, first]], source[sort_s[at + 1, second]])

    def take_received(stage, chunk):
        @pl.loop(0, PARTS, unroll=8)
        def _(p):
            pair = recv[stage, chunk, p]
            table[chunk, BLOCKS + 2 * p] = split(pair)
            table[chunk, BLOCKS + 2 * p + 1] = split(turn(pair))

    def products(stage, chunk):
        wait_received(stage, chunk)
        take_received(stage, chunk)
        half = SLOTS // 2
        for n in range(BLOCKS):
            for k in range(half):
                even = table[chunk, sort_s[0, n * half + k]]
                odd = table[chunk, sort_s[0, LIVE // 2 + n * half + k]]
                picked[n, :, k * PAIR : (k + 1) * PAIR] = jnp.where(low_half16, even, odd)
        for n in range(BLOCKS):
            parts[n] = jnp.dot(picked[n], across[n], preferred_element_type=jnp.float32)

    def value_of(chunk, n):
        both = parts[n, :ROWS] + parts[n, ROWS:]
        return both + turn(both) + exit_dup[chunk, n]

    def adjoint_message(stage, chunk):
        half = SLOTS // 2
        for n in range(BLOCKS):
            out = jnp.dot(ratios[n], matrix[n], preferred_element_type=jnp.float32)
            both = out[:ROWS] + out[ROWS:]
            for k in range(half):
                terms[n * half + k] = both[:, k * PAIR : (k + 1) * PAIR]
        run_sums(terms, keep, scan, 1, LIVE // 2)

        def make(i):
            one, two, three, four = (scan[sum_at[4 * i + j]] for j in range(4))
            return jnp.where(low_half, one, two) + turn(jnp.where(low_half, three, four))

        message(stage, chunk, make)
        for b in range(BLOCKS):
            own = sums_at(scan, 2, b, b)
            local[chunk, b] = own + turn(own)

    @pl.loop(0, CHUNKS)
    def _(chunk):
        products(0, chunk)
        for n in range(BLOCKS):
            weighted[n] = value_of(chunk, n) * scale_row(n)
        forward_message(1, chunk)
        own_table(chunk)

    @pl.loop(0, CHUNKS)
    def _(chunk):
        products(1, chunk)
        for n in range(BLOCKS):
            value = value_of(chunk, n)
            value_dup[chunk, n] = value
            ratio = demand_dup[chunk, n] / value
            ratio_dup[chunk, n] = ratio
            ratios[n] = split(ratio)
        adjoint_message(2, chunk)

    def gather_back(stage, chunk):
        wait_received(stage, chunk)
        for p in range(PARTS):
            returned[p] = recv[stage, chunk, p]
        run_sums(returned, back_keep, back_scan, 4, PARTS)

    def back_of(chunk, n):
        came = sums_at(back_scan, 5, n, n)
        return (local[chunk, n] + came + turn(came)) * scale_row(n)

    @pl.loop(0, CHUNKS)
    def _(chunk):
        gather_back(2, chunk)
        for n in range(BLOCKS):
            ratios[n] = split(back_of(chunk, n) + ratio_dup[chunk, n])
        adjoint_message(3, chunk)

    @pl.loop(0, CHUNKS)
    def _(chunk):
        gather_back(3, chunk)
        weight = dest_w[rows_of(chunk), :]
        for g in range(GROUPS):
            flow, grad = [], []
            for h in range(2):
                n = 2 * g + h
                moved = value_dup[chunk, n] * back_of(chunk, n)
                flow.append(jnp.sum(moved + demand_dup[chunk, n], axis=0, keepdims=True))
                grad.append(jnp.sum(weight * moved, axis=0, keepdims=True))
            z_part[g, 0:1, :] += jnp.where(low1, flow[0], flow[1]) / (DESTS * GROUPS)
            z_part[g, 1:2, :] -= jnp.where(low1, grad[0], grad[1]) / (DESTS * GROUPS)

    for dz in Z_OFFSETS:
        to = (group + dz) % GROUPS
        pltpu.make_async_remote_copy(
            src_ref=z_part.at[to],
            dst_ref=z_out.at[group],
            send_sem=z_send_sem,
            recv_sem=z_recv_sem,
            device_id=(me, to),
            device_id_type=MESH,
        ).start()
    own = pltpu.make_async_copy(z_part.at[group], z_out.at[group], z_own_sem)
    own.start()
    arrived = z_out.at[pl.ds(0, GROUPS - 1)]
    pltpu.make_async_copy(arrived, arrived, z_recv_sem).wait()
    own.wait()

    left = z_part.at[pl.ds(0, GROUPS - 1)]
    pltpu.make_async_copy(left, left, z_send_sem).wait()

    @pl.loop(0, STAGES)
    def _(stage):
        @pl.loop(0, CHUNKS)
        def _(chunk):
            gone = send.at[stage, chunk, pl.ds(0, PARTS - 1)]
            pltpu.make_async_copy(gone, gone, send_sem.at[stage, chunk]).wait()


def local_part(cost, turn_weight, exit_value, demand, dest_weight, slot_count, col_ref, send_blocks):
    anywhere = pl.BlockSpec(memory_space=pl.ANY)
    f32, bf16 = jnp.float32, jnp.bfloat16
    parts = pl.pallas_call(
        kernel,
        out_shape=jax.ShapeDtypeStruct((GROUPS, 2, PAIR), f32),
        in_specs=[anywhere] * 8,
        out_specs=anywhere,
        scratch_shapes=[
            pltpu.VMEM((BLOCKS, BLK, SLOTS * BLK), f32),
            pltpu.VMEM((DESTS, BLOCKS * BLK), f32),
            pltpu.VMEM((DESTS, BLOCKS * BLK), f32),
            pltpu.VMEM((BLOCKS * BLK,), f32),
            pltpu.SMEM((DESTS,), f32),
            pltpu.SMEM((BLOCKS,), jnp.int32),
            pltpu.SMEM((SLOTS, BLOCKS), jnp.int32),
            pltpu.SMEM((2, PARTS), jnp.int32),
            pltpu.VMEM((BLOCKS, 2 * BLK, SLOTS * BLK), bf16),
            pltpu.VMEM((BLOCKS, SLOTS * BLK, 2 * BLK), bf16),
            pltpu.VMEM((CHUNKS, BLOCKS + GHOSTS, 2 * ROWS, PAIR), bf16),
            pltpu.VMEM((BLOCKS, 2 * ROWS, SLOTS * BLK), bf16),
            pltpu.VMEM((BLOCKS, 2 * ROWS, PAIR), f32),
            pltpu.VMEM((BLOCKS, 2 * ROWS, PAIR), bf16),
            pltpu.VMEM((CHUNKS, BLOCKS, ROWS, PAIR), f32),
            pltpu.VMEM((BLOCKS, ROWS, PAIR), f32),
            pltpu.VMEM((CHUNKS, BLOCKS, ROWS, PAIR), f32),
            pltpu.VMEM((CHUNKS, BLOCKS, ROWS, PAIR), f32),
            pltpu.VMEM((CHUNKS, BLOCKS, ROWS, PAIR), f32),
            pltpu.VMEM((BLOCKS, PAIR), f32),
            pltpu.VMEM((DESTS, PAIR), f32),
            pltpu.VMEM((LIVE // 2, ROWS, PAIR), f32),
            pltpu.VMEM((LIVE // 2 + 1, ROWS, PAIR), f32),
            pltpu.VMEM((PARTS + 1, ROWS, PAIR), f32),
            pltpu.VMEM((LIVE // 2, PAIR), f32),
            pltpu.VMEM((PARTS, PAIR), f32),
            pltpu.VMEM((CHUNKS, BLOCKS, ROWS, PAIR), f32),
            pltpu.VMEM((PARTS, ROWS, PAIR), f32),
            pltpu.VMEM((8, 128), jnp.int32),
            pltpu.SMEM((8, 128), jnp.int32),
            pltpu.SMEM((2 * PARTS,), jnp.int32),
            pltpu.SMEM((4 * PARTS,), jnp.int32),
            pltpu.VMEM((STAGES, CHUNKS, PARTS, ROWS, PAIR), f32),
            pltpu.VMEM((STAGES, CHUNKS, PARTS, ROWS, PAIR), f32),
            pltpu.VMEM((GROUPS, 2, PAIR), f32),
            pltpu.SemaphoreType.DMA((8,)),
            pltpu.SemaphoreType.DMA((STAGES, CHUNKS)),
            pltpu.SemaphoreType.DMA((STAGES, CHUNKS)),
            pltpu.SemaphoreType.DMA,
            pltpu.SemaphoreType.DMA,
            pltpu.SemaphoreType.DMA,
        ],
        compiler_params=pltpu.CompilerParams(
            collective_id=0, has_side_effects=True, vmem_limit_bytes=60 * 2**20
        ),
        name="route_choice",
    )(
        cost, exit_value, demand, turn_weight, dest_weight, slot_count, col_ref.T,
        send_blocks.transpose(0, 2, 1),
    )
    return jnp.sum(parts[:, 0], axis=0), jnp.sum(parts[:, 1], axis=0)


def solution(mesh):
    placed = (
        P("dom"),
        P("dom", None, None),
        P("dest", "dom"),
        P("dest", "dom"),
        P("dest"),
        P("dom"),
        P("dom", None),
        P(),
    )
    return jax.shard_map(
        local_part,
        mesh=mesh,
        in_specs=placed,
        out_specs=(P(("dom", "dest")), P(("dom", "dest"))),
        check_vma=False,
    )
```

```python
import functools

import jax
import jax.numpy as jnp
from jax import lax
from jax.experimental import pallas as pl
from jax.experimental.pallas import tpu as pltpu
from jax.sharding import PartitionSpec as P

MESH = pl.DeviceIdType.MESH
BLK = 64
PAIR = 2 * BLK
SLOTS = 8
BLOCKS = 16
PARTS = 32
GROUPS = 8
DESTS = 48
CHUNKS = 3
ROWS = DESTS // CHUNKS
LIVE = BLOCKS * SLOTS
GHOSTS = 2 * PARTS
STAGES = 4


def hops(offset):
    dx, dy, _ = offset
    return min(dx, 4 - dx) + min(dy, 4 - dy)


OFFSETS = sorted(
    ((dx, dy, dc) for dx in range(4) for dy in range(4) for dc in range(2) if dx or dy or dc),
    key=lambda o: (-hops(o), o[2]),
)
Z_OFFSETS = (4, 3, 5, 2, 6, 1, 7)


def split(v):
    high = v.astype(jnp.bfloat16)
    low = (v - high.astype(jnp.float32)).astype(jnp.bfloat16)
    return jnp.concatenate([high, low], axis=0)


def turn(v):
    return pltpu.roll(v, BLK, 1)


def kernel(
    cost_hbm, exit_hbm, demand_hbm, turn_hbm, weight_hbm, count_hbm, col_hbm, send_blocks_hbm,
    z_out,
    turn_raw, exit_ref, demand_ref, cost_ref, weight_ref, count_ref, col_ref, outb_ref,
    matrix, across, table, picked, parts, ratios, exit_dup, weighted, value_dup, ratio_dup, demand_dup, scale, dest_w,
    terms, scan, back_scan, keep, back_keep, local, returned, sort_v, sort_s, out_at, sum_at,
    send, recv, z_part,
    load_sem, send_sem, recv_sem, z_send_sem, z_recv_sem, z_own_sem,
):
    me = lax.axis_index("dom")
    group = lax.axis_index("dest")
    x, y, c = me // 8, (me // 2) % 4, me % 2

    along_x = [8 * ((x + d) % 4) for d in range(4)]
    along_y = [2 * ((y + d) % 4) for d in range(4)]
    core = (c, 1 - c)

    def partner(offset):
        dx, dy, dc = offset
        return along_x[dx] + along_y[dy] + core[dc]

    loads = [
        pltpu.make_async_copy(source, target, load_sem.at[i])
        for i, (source, target) in enumerate(
            (
                (cost_hbm, cost_ref),
                (exit_hbm, exit_ref),
                (send_blocks_hbm.at[me], outb_ref),
                (turn_hbm, turn_raw),
                (demand_hbm, demand_ref),
                (col_hbm, col_ref),
                (count_hbm, count_ref),
                (weight_hbm, weight_ref),
            )
        )
    ]
    for load in loads[:3]:
        load.start()

    barrier = pltpu.get_barrier_semaphore()
    for offset in OFFSETS:
        pl.semaphore_signal(barrier, inc=1, device_id=(partner(offset), group), device_id_type=MESH)
    for dz in Z_OFFSETS:
        pl.semaphore_signal(barrier, inc=1, device_id=(me, (group + dz) % GROUPS), device_id_type=MESH)

    for load in loads[3:]:
        load.start()

    lane = lax.broadcasted_iota(jnp.int32, (ROWS, PAIR), 1)
    low_half = lane < BLK
    low_half16 = lax.broadcasted_iota(jnp.int32, (2 * ROWS, PAIR), 1) < BLK
    lane_row = lax.broadcasted_iota(jnp.int32, (1, PAIR), 1)
    low1 = lane_row < BLK

    def message(stage, chunk, make):
        for i, offset in enumerate(OFFSETS):
            to = partner(offset)
            send[stage, chunk, i] = make(i)
            pltpu.make_async_remote_copy(
                src_ref=send.at[stage, chunk, i],
                dst_ref=recv.at[stage, chunk, me],
                send_sem=send_sem.at[stage, chunk],
                recv_sem=recv_sem.at[stage, chunk],
                device_id=(to, group),
                device_id_type=MESH,
            ).start()
        recv[stage, chunk, me] = make(PARTS - 1)

    def wait_received(stage, chunk):
        here = recv.at[stage, chunk, pl.ds(0, PARTS - 1)]
        pltpu.make_async_copy(here, here, recv_sem.at[stage, chunk]).wait()

    def forward_message(stage, chunk):
        def make(i):
            return jnp.where(low_half, weighted[out_at[2 * i]], weighted[out_at[2 * i + 1]])

        message(stage, chunk, make)

    def own_table(chunk):
        for n in range(BLOCKS):
            table[chunk, n] = split(weighted[n])

    def scale_row(n):
        return scale[n : n + 1, :]

    def rows_of(chunk):
        return pl.ds(pl.multiple_of(chunk * ROWS, 8), ROWS)

    def start_first(chunk):
        for m in range(BLOCKS // 2):
            pair = exit_ref[rows_of(chunk), m * PAIR : (m + 1) * PAIR]
            other = turn(pair)
            for h in range(2):
                n = 2 * m + h
                dup = jnp.where(low_half, pair, other) if h == 0 else jnp.where(low_half, other, pair)
                exit_dup[chunk, n] = dup
                weighted[n] = dup * scale_row(n)

    loads[0].wait()
    for m in range(BLOCKS // 2):
        factor = jnp.exp(-cost_ref[pl.ds(m * PAIR, PAIR)].reshape(1, PAIR))
        turned = turn(factor)
        scale[2 * m : 2 * m + 1, :] = jnp.where(low1, factor, turned)
        scale[2 * m + 1 : 2 * m + 2, :] = jnp.where(low1, turned, factor)
    loads[2].wait()
    for i, offset in enumerate((*OFFSETS, (0, 0, 0))):
        to = partner(offset)
        for h in range(2):
            out_at[2 * i + h] = outb_ref[h, to]
    loads[1].wait()
    start_first(0)
    pl.semaphore_wait(barrier, len(OFFSETS) + len(Z_OFFSETS))
    forward_message(0, 0)
    own_table(0)

    @pl.loop(1, CHUNKS)
    def _(chunk):
        start_first(chunk)
        forward_message(0, chunk)
        own_table(chunk)

    for load in loads[3:]:
        load.wait()

    square_lane = lax.broadcasted_iota(jnp.int32, (128, 128), 1)
    square_row = lax.broadcasted_iota(jnp.int32, (128, 128), 0)

    def order(keys, half, at, keep_ref):
        odd = lane_row >= half
        row = jnp.where(lane_row < 2 * half, keys + jnp.where(odd, 256, 0), 4096)
        along = jnp.broadcast_to(row, (128, 128))
        down = along.T
        before = (along < down) | ((along == down) & (square_lane < square_row))
        rank = jnp.sum(jnp.where(before, 1, 0), axis=1, keepdims=True)
        hit = rank == square_lane
        entry = jnp.sum(jnp.where(hit, square_row, 0), axis=0, keepdims=True)
        key = jnp.sum(jnp.where(hit, down, 0), axis=0, keepdims=True)
        same = (key == pltpu.roll(key, 1, 1)) & (lane_row > 0)
        kept = jnp.broadcast_to(jnp.where(same, 1.0, 0.0), (128, 128)).T
        keep_ref[...] = jnp.where(low1, kept[:half], kept[half : 2 * half])
        sort_v[at : at + 1, :] = jnp.clip(entry - jnp.where(odd, half, 0), 0, half - 1)
        for h in range(2):
            target = square_lane + 256 * h
            upto = jnp.sum(jnp.where(down <= target, 1, 0), axis=0, keepdims=True)
            count = jnp.sum(jnp.where(down == target, 1, 0), axis=0, keepdims=True)
            last = jnp.where(count > 0, upto - 1 - half * h, half)
            sort_v[at + 1 + h : at + 2 + h, :] = jnp.clip(last, 0, half)

    def col_key(n, row):
        for s in range(SLOTS):
            at = (s % 2) * (LIVE // 2) + n * (SLOTS // 2) + s // 2
            row = jnp.where(lane_row == at, col_ref[s, n], row)
        return row

    def out_key(q, row):
        for h in range(2):
            row = jnp.where(lane_row == h * PARTS + q, outb_ref[h, q], row)
        return row

    col_row = lax.fori_loop(0, BLOCKS, col_key, jnp.zeros((1, 128), jnp.int32))
    out_row = lax.fori_loop(0, PARTS, out_key, jnp.zeros((1, 128), jnp.int32))
    sort_v[...] = jnp.zeros_like(sort_v)
    order(col_row, LIVE // 2, 1, keep)
    order(out_row, PARTS, 4, back_keep)
    swapped = (col_row >= BLOCKS) & (lane_row >= LIVE // 2)
    sort_v[0:1, :] = jnp.where(swapped, col_row + 1 - 2 * (col_row % 2), col_row)
    sort_copy = pltpu.make_async_copy(sort_v, sort_s, load_sem.at[0])
    sort_copy.start()

    @pl.loop(0, BLOCKS)
    def _(n):
        column = lax.broadcasted_iota(jnp.int32, (BLK, SLOTS * BLK), 1)
        live = jnp.where(column < count_ref[n] * BLK, turn_raw[n], 0.0)
        both = split(live)
        matrix[n] = both
        across[n] = both.T

    @pl.loop(0, CHUNKS)
    def _(chunk):
        for m in range(BLOCKS // 2):
            pair = demand_ref[rows_of(chunk), m * PAIR : (m + 1) * PAIR]
            other = turn(pair)
            demand_dup[chunk, 2 * m] = jnp.where(low_half, pair, other)
            demand_dup[chunk, 2 * m + 1] = jnp.where(low_half, other, pair)

    @pl.loop(0, DESTS)
    def _(d):
        dest_w[pl.ds(d, 1), :] = jnp.full((1, PAIR), weight_ref[d], jnp.float32)

    sort_copy.wait()
    for i, offset in enumerate((*OFFSETS, (0, 0, 0))):
        first = BLOCKS + 2 * partner(offset)
        sum_at[4 * i] = sort_s[2, first]
        sum_at[4 * i + 1] = sort_s[3, first + 1]
        sum_at[4 * i + 2] = sort_s[2, first + 1]
        sum_at[4 * i + 3] = sort_s[3, first]
    scan[LIVE // 2] = jnp.zeros((ROWS, PAIR), jnp.float32)
    back_scan[PARTS] = jnp.zeros((ROWS, PAIR), jnp.float32)
    z_part[...] = jnp.zeros_like(z_part)

    def run_sums(source, keep_ref, target, at, half):
        for k in range(half):
            found = jnp.where(low_half, source[sort_s[at, k]], source[sort_s[at, half + k]])
            running = found if k == 0 else found + keep_ref[k : k + 1, :] * running
            target[k] = running

    def sums_at(source, at, first, second):
        return jnp.where(low_half, source[sort_s[at, first]], source[sort_s[at + 1, second]])

    def take_received(stage, chunk):
        @pl.loop(0, PARTS, unroll=PARTS)
        def _(p):
            pair = recv[stage, chunk, p]
            table[chunk, BLOCKS + 2 * p] = split(pair)
            table[chunk, BLOCKS + 2 * p + 1] = split(turn(pair))

    def products(stage, chunk):
        wait_received(stage, chunk)
        take_received(stage, chunk)
        half = SLOTS // 2
        for n in range(BLOCKS):
            for k in range(half):
                even = table[chunk, sort_s[0, n * half + k]]
                odd = table[chunk, sort_s[0, LIVE // 2 + n * half + k]]
                picked[n, :, k * PAIR : (k + 1) * PAIR] = jnp.where(low_half16, even, odd)
        for n in range(BLOCKS):
            parts[n] = jnp.dot(picked[n], across[n], preferred_element_type=jnp.float32)

    def value_of(chunk, n):
        both = parts[n, :ROWS] + parts[n, ROWS:]
        return both + turn(both) + exit_dup[chunk, n]

    def adjoint_message(stage, chunk):
        half = SLOTS // 2
        for n in range(BLOCKS):
            out = jnp.dot(ratios[n], matrix[n], preferred_element_type=jnp.float32)
            both = out[:ROWS] + out[ROWS:]
            for k in range(half):
                terms[n * half + k] = both[:, k * PAIR : (k + 1) * PAIR]
        run_sums(terms, keep, scan, 1, LIVE // 2)

        def make(i):
            one, two, three, four = (scan[sum_at[4 * i + j]] for j in range(4))
            return jnp.where(low_half, one, two) + turn(jnp.where(low_half, three, four))

        message(stage, chunk, make)
        for b in range(BLOCKS):
            own = sums_at(scan, 2, b, b)
            local[chunk, b] = own + turn(own)

    @pl.loop(0, CHUNKS)
    def _(chunk):
        products(0, chunk)
        for n in range(BLOCKS):
            weighted[n] = value_of(chunk, n) * scale_row(n)
        forward_message(1, chunk)
        own_table(chunk)

    @pl.loop(0, CHUNKS)
    def _(chunk):
        products(1, chunk)
        for n in range(BLOCKS):
            value = value_of(chunk, n)
            value_dup[chunk, n] = value
            ratio = demand_dup[chunk, n] / value
            ratio_dup[chunk, n] = ratio
            ratios[n] = split(ratio)
        adjoint_message(2, chunk)

    def gather_back(stage, chunk):
        wait_received(stage, chunk)
        for p in range(PARTS):
            returned[p] = recv[stage, chunk, p]
        run_sums(returned, back_keep, back_scan, 4, PARTS)

    def back_of(chunk, n):
        came = sums_at(back_scan, 5, n, n)
        return (local[chunk, n] + came + turn(came)) * scale_row(n)

    @pl.loop(0, CHUNKS)
    def _(chunk):
        gather_back(2, chunk)
        for n in range(BLOCKS):
            ratios[n] = split(back_of(chunk, n) + ratio_dup[chunk, n])
        adjoint_message(3, chunk)

    @pl.loop(0, CHUNKS)
    def _(chunk):
        gather_back(3, chunk)
        weight = dest_w[rows_of(chunk), :]
        for g in range(GROUPS):
            flow, grad = [], []
            for h in range(2):
                n = 2 * g + h
                moved = value_dup[chunk, n] * back_of(chunk, n)
                flow.append(jnp.sum(moved + demand_dup[chunk, n], axis=0, keepdims=True))
                grad.append(jnp.sum(weight * moved, axis=0, keepdims=True))
            z_part[g, 0:1, :] += jnp.where(low1, flow[0], flow[1]) / (DESTS * GROUPS)
            z_part[g, 1:2, :] -= jnp.where(low1, grad[0], grad[1]) / (DESTS * GROUPS)

    for dz in Z_OFFSETS:
        to = (group + dz) % GROUPS
        pltpu.make_async_remote_copy(
            src_ref=z_part.at[to],
            dst_ref=z_out.at[group],
            send_sem=z_send_sem,
            recv_sem=z_recv_sem,
            device_id=(me, to),
            device_id_type=MESH,
        ).start()
    own = pltpu.make_async_copy(z_part.at[group], z_out.at[group], z_own_sem)
    own.start()
    arrived = z_out.at[pl.ds(0, GROUPS - 1)]
    pltpu.make_async_copy(arrived, arrived, z_recv_sem).wait()
    own.wait()

    left = z_part.at[pl.ds(0, GROUPS - 1)]
    pltpu.make_async_copy(left, left, z_send_sem).wait()

    @pl.loop(0, STAGES)
    def _(stage):
        @pl.loop(0, CHUNKS)
        def _(chunk):
            gone = send.at[stage, chunk, pl.ds(0, PARTS - 1)]
            pltpu.make_async_copy(gone, gone, send_sem.at[stage, chunk]).wait()


def local_part(cost, turn_weight, exit_value, demand, dest_weight, slot_count, col_ref, send_blocks):
    anywhere = pl.BlockSpec(memory_space=pl.ANY)
    f32, bf16 = jnp.float32, jnp.bfloat16
    parts = pl.pallas_call(
        kernel,
        out_shape=jax.ShapeDtypeStruct((GROUPS, 2, PAIR), f32),
        in_specs=[anywhere] * 8,
        out_specs=anywhere,
        scratch_shapes=[
            pltpu.VMEM((BLOCKS, BLK, SLOTS * BLK), f32),
            pltpu.VMEM((DESTS, BLOCKS * BLK), f32),
            pltpu.VMEM((DESTS, BLOCKS * BLK), f32),
            pltpu.VMEM((BLOCKS * BLK,), f32),
            pltpu.SMEM((DESTS,), f32),
            pltpu.SMEM((BLOCKS,), jnp.int32),
            pltpu.SMEM((SLOTS, BLOCKS), jnp.int32),
            pltpu.SMEM((2, PARTS), jnp.int32),
            pltpu.VMEM((BLOCKS, 2 * BLK, SLOTS * BLK), bf16),
            pltpu.VMEM((BLOCKS, SLOTS * BLK, 2 * BLK), bf16),
            pltpu.VMEM((CHUNKS, BLOCKS + GHOSTS, 2 * ROWS, PAIR), bf16),
            pltpu.VMEM((BLOCKS, 2 * ROWS, SLOTS * BLK), bf16),
            pltpu.VMEM((BLOCKS, 2 * ROWS, PAIR), f32),
            pltpu.VMEM((BLOCKS, 2 * ROWS, PAIR), bf16),
            pltpu.VMEM((CHUNKS, BLOCKS, ROWS, PAIR), f32),
            pltpu.VMEM((BLOCKS, ROWS, PAIR), f32),
            pltpu.VMEM((CHUNKS, BLOCKS, ROWS, PAIR), f32),
            pltpu.VMEM((CHUNKS, BLOCKS, ROWS, PAIR), f32),
            pltpu.VMEM((CHUNKS, BLOCKS, ROWS, PAIR), f32),
            pltpu.VMEM((BLOCKS, PAIR), f32),
            pltpu.VMEM((DESTS, PAIR), f32),
            pltpu.VMEM((LIVE // 2, ROWS, PAIR), f32),
            pltpu.VMEM((LIVE // 2 + 1, ROWS, PAIR), f32),
            pltpu.VMEM((PARTS + 1, ROWS, PAIR), f32),
            pltpu.VMEM((LIVE // 2, PAIR), f32),
            pltpu.VMEM((PARTS, PAIR), f32),
            pltpu.VMEM((CHUNKS, BLOCKS, ROWS, PAIR), f32),
            pltpu.VMEM((PARTS, ROWS, PAIR), f32),
            pltpu.VMEM((8, 128), jnp.int32),
            pltpu.SMEM((8, 128), jnp.int32),
            pltpu.SMEM((2 * PARTS,), jnp.int32),
            pltpu.SMEM((4 * PARTS,), jnp.int32),
            pltpu.VMEM((STAGES, CHUNKS, PARTS, ROWS, PAIR), f32),
            pltpu.VMEM((STAGES, CHUNKS, PARTS, ROWS, PAIR), f32),
            pltpu.VMEM((GROUPS, 2, PAIR), f32),
            pltpu.SemaphoreType.DMA((8,)),
            pltpu.SemaphoreType.DMA((STAGES, CHUNKS)),
            pltpu.SemaphoreType.DMA((STAGES, CHUNKS)),
            pltpu.SemaphoreType.DMA,
            pltpu.SemaphoreType.DMA,
            pltpu.SemaphoreType.DMA,
        ],
        compiler_params=pltpu.CompilerParams(
            collective_id=0, has_side_effects=True, vmem_limit_bytes=60 * 2**20
        ),
        name="route_choice",
    )(
        cost, exit_value, demand, turn_weight, dest_weight, slot_count, col_ref.T,
        send_blocks.transpose(0, 2, 1),
    )
    return jnp.sum(parts[:, 0], axis=0), jnp.sum(parts[:, 1], axis=0)


def solution(mesh):
    placed = (
        P("dom"),
        P("dom", None, None),
        P("dest", "dom"),
        P("dest", "dom"),
        P("dest"),
        P("dom"),
        P("dom", None),
        P(),
    )
    return jax.shard_map(
        local_part,
        mesh=mesh,
        in_specs=placed,
        out_specs=(P(("dom", "dest")), P(("dom", "dest"))),
        check_vma=False,
    )
```
